512 devices in a mesh: tm: 64 (over z, y), tensor: 8 (over x, core).
Axes of the slice: x: 4, y: 8, z: 8, core: 2. Of those that a mesh axis runs over, the one named last changes fastest.
Arguments:
- frames: bfloat16 [32768, 1024], P('tm', 'tensor'), may hold values from -16 to 16
- conv_kernel: bfloat16 [31, 1024], P(None, 'tensor'), may hold values from -1 to 1
- conv_gain: float32 [1024], P('tensor'), may hold values from 0.1 to 1.9
- ffn_gain: float32 [1024], P('tensor'), may hold values from 0.1 to 1.9
- lengths: int32 [8], replicated, may hold values from 1 to 8192, 32768 in all
- routes: int32 [32768, 2], P('tm'), may hold values from 0 to 63, all different within a row; in each aligned block of 512 rows (0 to 511, 512 to 1023, ...) at most 24 rows name the same one
- route_weights: float32 [32768, 2], P('tm'), may hold values from 0.2 to 1
- w_gate: bfloat16 [64, 1024, 4096], P('tm', None, 'tensor'), may hold values from -0.1875 to 0.1875
- w_up: bfloat16 [64, 1024, 4096], P('tm', None, 'tensor'), may hold values from -0.1875 to 0.1875
- w_down: bfloat16 [64, 4096, 1024], P('tm', 'tensor'), may hold values from -0.09375 to 0.09375
Outputs:
- block_out: bfloat16 [32768, 1024], P('tm', 'tensor')
The draws below stay inside these ranges and needn't reach their ends.
Inputs may be any that keep to these rules, and one draw needn't show every extreme that they name: `routes`: each row names 2 different experts. Among the 512 rows of one device, no expert is named more than 24 times, and in every draw some expert is named exactly 24 times there. The lengths sum to 32768; the largest is exactly 8192.
All inputs are finite; a program needn't handle non-finite values.
Results may differ from the reference program's by a relative error of at most 0.007.
Values may be sent and summed in bfloat16 or wider, within the bound.
A program may use at most 64 MiB of HBM per device.

```python
import math
import jax
import jax.numpy as jnp
import numpy as np
from jax import lax

D = 1024
FF = 4096
KERNEL = 31
TOP = 2
UTTS = 8
F_DEV = 512
EXPERTS = 64
CAP = 24
FRAMES = 32768
N_TM = 64
N_TENSOR = 8


def draw_frames(key, part):
    key = jax.random.fold_in(key, 11)
    first, second = jax.random.split(key, 2)
    channel = 3.0 ** (jnp.arange(D, dtype=jnp.float32) / D) * jax.random.uniform(second, (D,), jnp.float32, 0.6, 1.4)
    value = jax.random.normal(first, (FRAMES, D), jnp.float32) * channel[None, :]
    return jnp.clip(value, -16.0, 16.0).astype(jnp.bfloat16)


def steps_of(stream_key, dims, cuts, smallest, largest):
    level = 1.0
    for axis_at, shards_of in cuts:
        draws = jax.random.uniform(jax.random.fold_in(jax.random.fold_in(stream_key, 6), axis_at), (shards_of,), jnp.float32, smallest / len(cuts), largest / len(cuts))
        level = level * jnp.repeat(jnp.exp(draws), dims[axis_at] // shards_of).reshape((-1,) + (1,) * (len(dims) - 1 - axis_at))
    return level


def split_up(count, total, limit, skew):
    weights = [(1 << 20) // math.isqrt(rank ** skew) + 1 for rank in range(2, count + 1)]
    spare, holding = total - limit - (count - 1), [1] * (count - 1)
    while spare > 0:
        free = [i for i in range(count - 1) if holding[i] < limit]
        whole, budget = sum([weights[i] for i in free]), spare
        for i in free:
            more = min(limit - holding[i], max(1, budget * weights[i] // whole), spare)
            holding[i] = holding[i] + more
            spare = spare - more
    return np.array([limit] + holding)


def ragged_sizes(stream_key, number_of, total, most, lean):
    if number_of == 2:
        one = jax.random.randint(stream_key, (), max(1, total - most), min(most, total - 1) + 1)
        return jnp.stack([one, total - one])
    sizes = jnp.asarray(split_up(number_of, total, most, lean), jnp.int32)
    couples = (number_of - 1) // 2
    source_of, taker = sizes[1:1 + 2 * couples:2], sizes[2:2 + 2 * couples:2]
    margin = jnp.minimum(source_of - 1, most - taker)
    shifted = jax.random.randint(jax.random.fold_in(stream_key, 1), (couples,), 0, 1 << 20) % (margin + 1)
    sizes = sizes.at[1:1 + 2 * couples:2].set(source_of - shifted).at[2:2 + 2 * couples:2].set(taker + shifted)
    return sizes[jax.random.permutation(jax.random.fold_in(stream_key, 2), number_of)]


def routed_block(rng, own, number, rows, amount, top, most, slope):
    order = jax.random.permutation(rng, amount)
    crowded, common = shares(amount, rows * top, most, slope, True), shares(amount, rows * top, most, slope, False)
    places = jnp.arange(amount)

    def named(tallies, rotation):
        used = int((tallies > 0).sum())
        fixed = max(1, used // 4)
        moved = fixed + (places - fixed + rotation * (used - fixed)) % max(1, amount - fixed)
        return jnp.zeros((amount,), jnp.int32).at[order[jnp.where(places < fixed, places, moved)]].set(jnp.asarray(tallies, jnp.int32))

    tallies = jnp.where(number % 4 == 0, named(crowded, number // 4), named(common, number - number // 4 - 1))
    mixed = jax.random.permutation(jax.random.fold_in(own, 3), amount)
    donor, sink = mixed[0:amount // 2 * 2:2], mixed[1:amount // 2 * 2:2]
    room = jnp.minimum(tallies[donor] - 1, most - tallies[sink]) // 2
    room = jnp.where((donor == order[0]) | (sink == order[0]) | (tallies[sink] == 0), 0, jnp.maximum(room, 0))
    moved = jax.random.randint(jax.random.fold_in(own, 4), (amount // 2,), 0, 1 << 20) % (room + 1)
    tallies = tallies.at[donor].add(-moved).at[sink].add(moved)
    labels = jnp.searchsorted(jnp.cumsum(tallies), jnp.arange(rows * top), side="right").astype(jnp.int32)
    table = labels.reshape(top, rows).T
    table = table[jax.random.permutation(jax.random.fold_in(own, 1), rows)]
    rotation = jax.random.randint(jax.random.fold_in(own, 2), (rows, 1), 0, top)
    return jnp.take_along_axis(table, (jnp.arange(top)[None, :] + rotation) % top, axis=1)


def shares(count, total, limit, skew, full):
    loads = [(1 << 20) // math.isqrt(grade ** skew) + 1 for grade in range(1, count + 1)]
    largest = limit if full else min(limit, max(-(-total // count), total * loads[0] // sum(loads)))
    least = 1 if total - largest >= count - 1 else 0
    given, surplus = [largest] + [least] * (count - 1), total - largest - least * (count - 1)
    while surplus > 0:
        free = [i for i in range(1, count) if given[i] < largest] or [i for i in range(1, count) if given[i] < limit]
        pool, left = sum([loads[i] for i in free]), surplus
        for i in free:
            more = min(limit - given[i], max(1, left * loads[i] // pool), surplus)
            given[i] = given[i] + more
            surplus = surplus - more
    return np.array(given)


def noise(key, dims, scale, most, pieces=(), held_as=jnp.bfloat16):
    result = jax.random.normal(key, dims, jnp.float32) * scale
    if len(pieces) > 0:
        result = steps_of(key, dims, pieces, -0.22, 0.18) * result
    return jnp.clip(result, min=-most, max=most).astype(held_as)


def setup_inputs(seed: int = 0) -> dict:
    splits = jax.random.split(jax.random.key(seed), 11)
    frames = draw_frames(jax.random.fold_in(splits[10], 71), 0)
    conv_kernel = noise(splits[1], (KERNEL, D), KERNEL ** -0.5, 1.0, ((1, 8),))
    conv_gain = jnp.clip(1.0 + 0.18 * jax.random.normal(splits[2], (D,), jnp.float32), 0.1, 1.9)
    ffn_gain = jnp.clip(1.0 + 0.18 * jax.random.normal(splits[3], (D,), jnp.float32), 0.1, 1.9)
    lengths = ragged_sizes(splits[4], UTTS, FRAMES, FRAMES // 4, 1).astype(jnp.int32)
    routes_keys = jax.random.split(jax.random.fold_in(splits[5], 1), FRAMES // F_DEV)
    routes_turns = jax.random.permutation(jax.random.fold_in(splits[5], 3), FRAMES // F_DEV)
    routes = jax.vmap(lambda own, number: routed_block(jax.random.fold_in(splits[5], 2), own, number, F_DEV, EXPERTS, TOP, CAP, 2))(routes_keys, routes_turns).reshape((FRAMES, TOP))
    route_weights = jnp.clip(0.2 + 0.8 * jax.random.uniform(splits[6], (FRAMES, TOP), jnp.float32) ** steps_of(splits[6], (FRAMES, TOP), ((0, 64),), -0.2, 0.2), 0.2, 1.0)
    w_gate = noise(splits[7], (EXPERTS, D, FF), D ** -0.5, 0.1875, ((0, 64), (2, 8)))
    w_up = noise(splits[8], (EXPERTS, D, FF), D ** -0.5, 0.1875, ((0, 64), (2, 8)))
    w_down = noise(splits[9], (EXPERTS, FF, D), FF ** -0.5, 0.09375, ((0, 64), (1, 8)))
    return {"frames": frames, "conv_kernel": conv_kernel, "conv_gain": conv_gain, "ffn_gain": ffn_gain, "lengths": lengths, "routes": routes, "route_weights": route_weights, "w_gate": w_gate, "w_up": w_up, "w_down": w_down}


eps = 1e-05

def layer_norm(value, gain):
    mean = lax.optimization_barrier(jnp.mean(value, axis=1, keepdims=True))
    square = lax.optimization_barrier(jnp.mean(value * value, axis=1, keepdims=True))
    return (value - mean) * lax.rsqrt(square - mean * mean + eps) * gain

def segment_ids(position, lengths):
    starts = jnp.cumsum(lengths) - lengths
    return lax.optimization_barrier(jnp.sum((position[:, None] >= starts[None, 1:]).astype(jnp.int32), axis=1))

def block_slots(names):
    onehot = (names[:, None] == jnp.arange(EXPERTS, dtype=jnp.int32)[None, :]).astype(jnp.int32)
    before = jnp.cumsum(onehot, axis=0) - onehot
    return (names * CAP + lax.optimization_barrier(jnp.sum(before * onehot, axis=1))).astype(jnp.int32)

def reference(frames, conv_kernel, conv_gain, ffn_gain, lengths, routes, route_weights, w_gate, w_up, w_down):
    x = frames.astype(jnp.float32)
    normed = layer_norm(x, conv_gain).astype(jnp.bfloat16)
    half = (KERNEL - 1) // 2
    position = jnp.arange(FRAMES + 2 * half, dtype=jnp.int32) - half
    segment = segment_ids(position, lengths)
    padded = jnp.pad(normed.astype(jnp.float32), ((half, half), (0, 0)))
    kernel = conv_kernel.astype(jnp.float32)
    own = segment[half:half + FRAMES]
    conv = jnp.zeros((FRAMES, D), jnp.float32)
    for tap in range(KERNEL):
        same = own == segment[tap:tap + FRAMES]
        conv = conv + jnp.where(same[:, None], padded[tap:tap + FRAMES] * kernel[tap], 0.0)
    resid = x + jax.nn.silu(conv)
    expert_in = layer_norm(resid, ffn_gain).astype(jnp.bfloat16)
    slots = jax.vmap(block_slots)(routes.reshape(N_TM, F_DEV * TOP))
    sources = jnp.repeat(expert_in.reshape(N_TM, F_DEV, D), TOP, axis=1)

    def place(slot_row, source_rows):
        return jnp.zeros((EXPERTS * CAP, D), jnp.bfloat16).at[slot_row].set(source_rows)
    buffers = jax.vmap(place)(slots, sources).reshape(N_TM, EXPERTS, CAP, D)
    buffers = jnp.transpose(buffers, (1, 0, 2, 3)).reshape(EXPERTS, N_TM * CAP, D)
    part = FF // N_TENSOR

    def expert(operands):
        rows, gate_w, up_w, down_w = operands
        gate = jnp.dot(rows, gate_w, preferred_element_type=jnp.float32)
        up = jnp.dot(rows, up_w, preferred_element_type=jnp.float32)
        hidden = (jax.nn.silu(gate) * up).astype(jnp.bfloat16)
        total = jnp.zeros((rows.shape[0], D), jnp.float32)
        for block in range(N_TENSOR):
            piece = jnp.dot(hidden[:, block * part:(block + 1) * part], down_w[block * part:(block + 1) * part], preferred_element_type=jnp.float32)
            total = total + lax.optimization_barrier(piece.astype(jnp.bfloat16)).astype(jnp.float32)
        return total.astype(jnp.bfloat16)
    outputs = lax.map(expert, (buffers, w_gate, w_up, w_down))
    outputs = jnp.transpose(outputs.reshape(EXPERTS, N_TM, CAP, D), (1, 0, 2, 3)).reshape(N_TM, EXPERTS * CAP, D)
    picked = jax.vmap(lambda table, slot_row: table[slot_row])(outputs, slots)
    picked = picked.reshape(FRAMES, TOP, D).astype(jnp.float32)
    mixed = resid + lax.optimization_barrier(jnp.sum(route_weights[:, :, None] * picked, axis=1))
    return mixed.astype(jnp.bfloat16)
```

```python
import functools
import types

import jax
import jax.numpy as jnp
from jax import lax
from jax.experimental import pallas as pl
from jax.experimental.pallas import tpu as pltpu
from jax.sharding import PartitionSpec as P

MESH = pl.DeviceIdType.MESH
EPS = 1e-05
CAP = 24
NX = 4
NZ = 8
NY = 8
F32 = jnp.float32
BF16 = jnp.bfloat16
I32 = jnp.int32


def div(a, b):
    return lax.div(a, jnp.int32(b))


def rem(a, b):
    return lax.rem(a, jnp.int32(b))


def remote(src, dst, ss, rs, dev):
    return pltpu.make_async_remote_copy(
        src_ref=src, dst_ref=dst, send_sem=ss, recv_sem=rs, device_id=dev, device_id_type=MESH
    )


def spread(row):
    return jnp.broadcast_to(row, (128, 128)).T


def row_sums(value_ref, dst_ref, groups):
    for g in range(groups):
        v = value_ref[128 * g : 128 * (g + 1), :].astype(F32).T
        dst_ref[g : g + 1, :] = jnp.sum(v, axis=0, keepdims=True)
        dst_ref[groups + g : groups + g + 1, :] = jnp.sum(v * v, axis=0, keepdims=True)


def names(rows, width, hid, depth, taps):
    groups = rows // 128
    chunks, per = NZ // 2, NY
    q = chunks * per
    crow = per * CAP
    hrow = crow // 2
    model = width * 2 * NX
    vm = pltpu.VMEM
    sem = pltpu.SemaphoreType.DMA
    return {
        "stat_s": vm((2, 2 * groups, 128), F32),
        "stat_r": vm((2, 2 * NX - 1, 2 * groups, 128), F32),
        "gain_s": vm((8, 128), F32),
        "gain_r": vm((8, 128), F32),
        "nbuf": vm((rows + 32, 128), F32),
        "halo_s": vm((2, 16, 128), BF16),
        "halo_r": vm((2, 16, 128), BF16),
        "behind": vm((rows, 128), I32),
        "ahead": vm((rows, 128), I32),
        "tapf": vm((32, 128), F32),
        "resid": vm((rows, 128), F32),
        "resid_p": vm((rows, 128), F32),
        "ein": vm((2, rows, 128), BF16),
        "pmat": vm((chunks, crow, rows), BF16),
        "dcol": vm((2, rows, 128), I32),
        "wcol": vm((2, rows, 128), F32),
        "wmat": vm((chunks, 2, rows, crow), BF16),
        "table": vm((q, 2 * CAP, 128), BF16),
        "gath": vm((NX, q, 2 * CAP, 128), BF16),
        "wg": vm((2, model, hid), BF16),
        "wu": vm((2, model, hid), BF16),
        "wd": vm((2, hid, model), BF16),
        "abuf": vm((crow, model), BF16),
        "hbuf": vm((crow, 2 * hid), BF16),
        "ybuf": vm((chunks, NX, crow, 256), F32),
        "rs_s": vm((chunks, 2, 3, hrow, 256), BF16),
        "rs_r": vm((chunks, 2, 3, hrow, 256), BF16),
        "back": vm((q, 2 * CAP, 128), BF16),
        "ret": vm((q, 2 * CAP, 128), BF16),
        "macc": vm((2, rows, 128), F32),
        "mix_r": vm((rows, 128), F32),
        "st_ss": sem((2, 2 * NX - 1)),
        "st_rs": sem((2, 2 * NX - 1)),
        "one_ss": sem((3,)),
        "one_rs": sem((3,)),
        "halo_ss": sem((2,)),
        "halo_rs": sem((2,)),
        "wl": sem((3,)),
        "w_ss": sem((3,)),
        "w_rs": sem((3,)),
        "a_ss": sem((q,)),
        "a_rs": sem((q,)),
        "g_ss": sem((chunks, 4)),
        "g_rs": sem((chunks, 4)),
        "r_ss": sem((chunks, 2, 3)),
        "r_rs": sem((chunks, 2, 3)),
        "b_ss": sem((q,)),
        "b_rs": sem((q,)),
    }


def kernel(keys, *refs):
    lengths_ref, frames_ref, taps_ref, cgain_ref, fgain_ref, routes_ref, rw_ref, wg_hbm, wu_hbm, wd_hbm, out_ref = refs[:11]
    s = types.SimpleNamespace(**dict(zip(keys, refs[11:])))
    rows, width = frames_ref.shape
    taps = taps_ref.shape[0]
    half = (taps - 1) // 2
    n_tm = NZ * NY
    n_t = 2 * NX
    model = width * n_t
    chunks = NZ // 2
    per = NY
    crow = per * CAP
    hrow = crow // 2
    groups = rows // 128

    tm = lax.axis_index("tm")
    ten = lax.axis_index("tensor")
    mz, my = div(tm, NY), rem(tm, NY)
    mx, mc = div(ten, 2), rem(ten, 2)
    oc = 1 - mc
    par = rem(my + mc, 2)
    xr, xl, xo = rem(mx + 1, NX), rem(mx + NX - 1, NX), rem(mx + 2, NX)
    peer_t = mx * 2 + rem(my, 2)
    partner = (tm, mx * 2 + oc)
    right, left = (tm, xr * 2 + mc), (tm, xl * 2 + mc)
    after, before = (rem(tm + 1, n_tm), ten), (rem(tm + n_tm - 1, n_tm), ten)

    def offsets(q):
        k, i = div(q, per), rem(q, per)
        return k + chunks * div(i, NY // 2), 2 * rem(i, NY // 2) + par

    def dest(q):
        dz, dy = offsets(q)
        return (rem(mz + dz, NZ) * NY + rem(my + dy, NY), peer_t)

    def source(q):
        dz, dy = offsets(q)
        return (rem(mz + NZ - dz, NZ) * NY + rem(my + NY - dy, NY), peer_t)

    def tensor_peer(d):
        return (tm, rem(ten + d, n_t))

    bar = pltpu.get_barrier_semaphore()

    def greet(dev):
        pl.semaphore_signal(bar, inc=1, device_id=dev, device_id_type=MESH)

    for d in range(1, n_t):
        greet(tensor_peer(d))
    greet(after)
    greet(before)

    @pl.loop(0, chunks * per)
    def _(q):
        @pl.when(q + par > 0)
        def _():
            greet(dest(q))

    hbm = (wg_hbm, wu_hbm, wd_hbm)
    wbuf = (s.wg, s.wu, s.wd)
    local_w = [pltpu.make_async_copy(hbm[i], wbuf[i].at[0], s.wl.at[i]) for i in range(3)]
    for copy in local_w:
        copy.start()
    row_sums(frames_ref, s.stat_s.at[0], groups)
    s.gain_s[...] = jnp.broadcast_to(fgain_ref[...], (8, 128))
    pl.semaphore_wait(bar, n_t - 1 + 2 + chunks * per - 1 + par)

    def stat_copies(phase):
        return [
            remote(s.stat_s.at[phase], s.stat_r.at[phase, d - 1], s.st_ss.at[phase, d - 1], s.st_rs.at[phase, d - 1], tensor_peer(d))
            for d in range(1, n_t)
        ]

    def norm_factors(phase):
        total = s.stat_s[phase]
        for d in range(n_t - 1):
            total = total + s.stat_r[phase, d]
        mean = total[0:groups] / model
        square = total[groups : 2 * groups] / model
        return mean, lax.rsqrt(square - mean * mean + EPS)

    first_stats = stat_copies(0)
    for copy in first_stats:
        copy.start()
    gain_copy = remote(s.gain_s, s.gain_r, s.one_ss.at[0], s.one_rs.at[0], partner)
    gain_copy.start()
    remote_w = [remote(hbm[i], wbuf[i].at[1], s.w_ss.at[i], s.w_rs.at[i], partner) for i in range(3)]
    for copy in remote_w:
        copy.start()

    s.tapf[0:taps, :] = taps_ref[...].astype(F32)
    starts = [jnp.int32(0)]
    for i in range(lengths_ref.shape[0]):
        starts.append(starts[-1] + lengths_ref[i])

    @pl.loop(0, groups)
    def _(g):
        r0 = pl.multiple_of(g * 128, 128)
        pos = tm * rows + r0 + lax.broadcasted_iota(I32, (128, 128), 0)
        begin = jnp.zeros((128, 128), I32)
        end = jnp.full((128, 128), n_tm * rows, I32)
        for i in range(1, len(starts) - 1):
            begin = jnp.where(pos >= starts[i], starts[i], begin)
        for i in range(len(starts) - 2, 0, -1):
            end = jnp.where(pos < starts[i], starts[i], end)
        s.behind[pl.ds(r0, 128), :] = pos - begin
        s.ahead[pl.ds(r0, 128), :] = end - 1 - pos

    n_exp = n_tm
    names_k = [routes_ref[0:1, :], routes_ref[1:2, :]]
    experts = lax.broadcasted_iota(I32, (n_exp, rows), 0)
    hot = [experts == name for name in names_k]
    both = jnp.where(hot[0] | hot[1], 1.0, 0.0).astype(BF16)
    upper = jnp.where(
        lax.broadcasted_iota(I32, (rows, rows), 0) < lax.broadcasted_iota(I32, (rows, rows), 1), 1.0, 0.0
    ).astype(BF16)
    earlier = jnp.dot(both, upper, preferred_element_type=F32)
    target = []
    for k in range(2):
        slot = jnp.sum(jnp.where(hot[k], earlier, 0.0), axis=0, keepdims=True).astype(I32)
        ez, ey = names_k[k] >> 3, names_k[k] & 7
        dz = (ez - mz + NZ) & (NZ - 1)
        dy = (ey - my + NY) & (NY - 1)
        q = (dz & (chunks - 1)) * per + (dz // chunks) * (NY // 2) + (dy >> 1)
        target.append(jnp.where((dy & 1) == par, q * CAP + slot, -1))
    place = lax.broadcasted_iota(I32, (crow, rows), 0)

    @pl.loop(0, chunks)
    def _(k):
        here = place + k * crow
        s.pmat[k] = jnp.where((here == target[0]) | (here == target[1]), 1.0, 0.0).astype(BF16)

    for copy in first_stats:
        copy.wait_recv()

    mean, scale = norm_factors(0)
    for g in range(groups):
        x = frames_ref[128 * g : 128 * (g + 1), :].astype(F32)
        n = ((x - spread(mean[g : g + 1])) * spread(scale[g : g + 1]) * cgain_ref[...]).astype(BF16)
        s.nbuf[16 + 128 * g : 16 + 128 * (g + 1), :] = n.astype(F32)
    s.halo_s[0] = s.nbuf[16:32, :].astype(BF16)
    s.halo_s[1] = s.nbuf[rows : rows + 16, :].astype(BF16)
    halos = [
        remote(s.halo_s.at[0], s.halo_r.at[0], s.halo_ss.at[0], s.halo_rs.at[0], before),
        remote(s.halo_s.at[1], s.halo_r.at[1], s.halo_ss.at[1], s.halo_rs.at[1], after),
    ]
    for copy in halos:
        copy.start()

    block = 64

    def conv(r0):
        acc = jnp.zeros((block, 128), F32)
        back_n = s.behind[pl.ds(r0, block), :]
        ahead_n = s.ahead[pl.ds(r0, block), :]
        for j in range(taps):
            d = j - half
            term = s.nbuf[pl.ds(r0 + 16 + d, block), :] * s.tapf[j : j + 1, :]
            if d < 0:
                term = jnp.where(back_n >= -d, term, 0.0)
            if d > 0:
                term = jnp.where(ahead_n >= d, term, 0.0)
            acc = acc + term
        x = frames_ref[pl.ds(r0, block), :].astype(F32)
        s.resid[pl.ds(r0, block), :] = x + acc / (1.0 + jnp.exp(-acc))

    for r0 in range(block, rows - block, block):
        conv(r0)
    for copy in halos:
        copy.wait_recv()
    s.nbuf[0:16, :] = s.halo_r[1].astype(F32)
    s.nbuf[rows + 16 : rows + 32, :] = s.halo_r[0].astype(F32)
    conv(0)
    conv(rows - block)

    resid_copy = remote(s.resid, s.resid_p, s.one_ss.at[1], s.one_rs.at[1], partner)
    resid_copy.start()
    row_sums(s.resid, s.stat_s.at[1], groups)
    second_stats = stat_copies(1)
    for copy in second_stats:
        copy.start()

    for k in range(2):
        for g in range(groups):
            lanes = slice(128 * g, 128 * (g + 1))
            s.dcol[k, lanes, :] = spread(target[k][:, lanes].astype(F32)).astype(I32)
            s.wcol[k, lanes, :] = spread(rw_ref[k : k + 1, lanes])

    gain_copy.wait_recv()
    resid_copy.wait_recv()
    for copy in second_stats:
        copy.wait_recv()
    mean, scale = norm_factors(1)
    for g in range(groups):
        m, r = spread(mean[g : g + 1]), spread(scale[g : g + 1])
        lanes = pl.ds(128 * g, 128)
        s.ein[mc, lanes, :] = ((s.resid[lanes, :] - m) * r * fgain_ref[...]).astype(BF16)
        s.ein[oc, lanes, :] = ((s.resid_p[lanes, :] - m) * r * s.gain_r[0:1, :]).astype(BF16)

    def send(q):
        return remote(s.table.at[q], s.gath.at[mx, q], s.a_ss.at[q], s.a_rs.at[q], dest(q))

    def keep(q):
        return pltpu.make_async_copy(s.table.at[q], s.gath.at[mx, q], s.a_rs.at[q])

    def pack(value):
        v = jnp.concatenate([value[:, 0:128].reshape(per, CAP, 128), value[:, 128:256].reshape(per, CAP, 128)], axis=1)
        return v.astype(BF16)

    def unpack(value):
        v = value.astype(F32)
        return v[:, :CAP, :].reshape(crow, 128).astype(BF16), v[:, CAP:, :].reshape(crow, 128).astype(BF16)

    def per_block(k, remotely, locally):
        @pl.loop(k * per, (k + 1) * per)
        def _(q):
            @pl.when(q + par > 0)
            def _():
                remotely(q)

            @pl.when(q + par == 0)
            def _():
                locally(q)

    @pl.loop(0, chunks)
    def _(k):
        both_cols = jnp.concatenate([s.ein[0], s.ein[1]], axis=1)
        picked = jnp.dot(s.pmat[k], both_cols, preferred_element_type=F32)
        s.table[pl.ds(k * per, per)] = pack(picked)
        per_block(k, lambda q: send(q).start(), lambda q: keep(q).start())

    @pl.loop(0, chunks)
    def _(k):
        here = k * crow + lax.broadcasted_iota(I32, (128, crow), 1)
        for g in range(groups):
            lanes = slice(128 * g, 128 * (g + 1))
            w = jnp.where(here == s.dcol[0, lanes, 0:1], s.wcol[0, lanes, 0:1], 0.0)
            w = w + jnp.where(here == s.dcol[1, lanes, 0:1], s.wcol[1, lanes, 0:1], 0.0)
            high = w.astype(BF16)
            s.wmat[k, 0, lanes, :] = high
            s.wmat[k, 1, lanes, :] = (w - high.astype(F32)).astype(BF16)

    s.macc[...] = jnp.zeros(s.macc.shape, F32)

    def gather_copies(k):
        whole, first, second = pl.ds(k * per, per), pl.ds(k * per, per // 2), pl.ds(k * per + per // 2, per // 2)

        def along(x, span, i, dev):
            return remote(s.gath.at[x, span], s.gath.at[x, span], s.g_ss.at[k, i], s.g_rs.at[k, i], dev)

        return (
            along(mx, whole, 0, right),
            along(mx, whole, 1, left),
            along(xl, first, 2, right),
            along(xr, second, 3, left),
        )

    def sum_copy(k, way, i):
        return remote(s.rs_s.at[k, way, i], s.rs_r.at[k, way, i], s.r_ss.at[k, way, i], s.r_rs.at[k, way, i], (right, left)[way])

    def send_back(q):
        return remote(s.back.at[q], s.ret.at[q], s.b_ss.at[q], s.b_rs.at[q], source(q))

    def keep_back(q):
        return pltpu.make_async_copy(s.back.at[q], s.ret.at[q], s.b_rs.at[q])

    for copy in local_w:
        copy.wait()
    for copy in remote_w:
        copy.wait_recv()

    def arrive(k):
        per_block(k, lambda q: send(q).wait_recv(), lambda q: keep(q).wait())
        to_right, to_left, _, _ = gather_copies(k)
        to_right.start()
        to_left.start()

    def forward(k):
        to_right, to_left, on_right, on_left = gather_copies(k)
        to_right.wait_recv()
        on_right.start()
        to_left.wait_recv()
        on_left.start()

    def experts_of(k):
        _, _, on_right, on_left = gather_copies(k)
        on_right.wait_recv()
        on_left.wait_recv()
        for x in range(NX):
            low, high = unpack(s.gath[x, pl.ds(k * per, per)])
            s.abuf[:, 256 * x : 256 * x + 128] = low
            s.abuf[:, 256 * x + 128 : 256 * x + 256] = high
        hid = s.wg.shape[2]
        for c in range(2):
            for n in range(0, hid, 256):
                gate = jnp.dot(s.abuf[...], s.wg[c, :, n : n + 256], preferred_element_type=F32)
                up = jnp.dot(s.abuf[...], s.wu[c, :, n : n + 256], preferred_element_type=F32)
                s.hbuf[:, hid * c + n : hid * c + n + 256] = (gate / (1.0 + jnp.exp(-gate)) * up).astype(BF16)
        for n in range(NX):
            cols = slice(256 * n, 256 * (n + 1))
            y = jnp.dot(s.hbuf[:, :hid], s.wd[0, :, cols], preferred_element_type=F32)
            s.ybuf[k, n] = y + jnp.dot(s.hbuf[:, hid:], s.wd[1, :, cols], preferred_element_type=F32)
        s.rs_s[k, 0, 0] = s.ybuf[k, xo, 0:hrow, :].astype(BF16)
        sum_copy(k, 0, 0).start()
        s.rs_s[k, 1, 0] = s.ybuf[k, xo, hrow:crow, :].astype(BF16)
        sum_copy(k, 1, 0).start()
        s.rs_s[k, 0, 1] = s.ybuf[k, xr, hrow:crow, :].astype(BF16)
        sum_copy(k, 0, 1).start()
        s.rs_s[k, 1, 1] = s.ybuf[k, xl, 0:hrow, :].astype(BF16)
        sum_copy(k, 1, 1).start()

    def pass_on(k):
        sum_copy(k, 0, 0).wait_recv()
        s.rs_s[k, 0, 2] = (s.ybuf[k, xr, 0:hrow, :] + s.rs_r[k, 0, 0].astype(F32)).astype(BF16)
        sum_copy(k, 0, 2).start()
        sum_copy(k, 1, 0).wait_recv()
        s.rs_s[k, 1, 2] = (s.ybuf[k, xl, hrow:crow, :] + s.rs_r[k, 1, 0].astype(F32)).astype(BF16)
        sum_copy(k, 1, 2).start()

    def finish(k):
        for way in range(2):
            sum_copy(k, way, 1).wait_recv()
            sum_copy(k, way, 2).wait_recv()
        top = s.ybuf[k, mx, 0:hrow, :] + s.rs_r[k, 0, 2].astype(F32) + s.rs_r[k, 1, 1].astype(F32)
        low = s.ybuf[k, mx, hrow:crow, :] + s.rs_r[k, 1, 2].astype(F32) + s.rs_r[k, 0, 1].astype(F32)
        s.back[pl.ds(k * per, per)] = pack(jnp.concatenate([top, low], axis=0))
        per_block(k, lambda q: send_back(q).start(), lambda q: keep_back(q).start())

    def combine(k):
        per_block(k, lambda q: send_back(q).wait_recv(), lambda q: keep_back(q).wait())
        low, high = unpack(s.ret[pl.ds(k * per, per)])
        both_cols = jnp.concatenate([low, high], axis=1)
        mixed = jnp.dot(s.wmat[k, 0], both_cols, preferred_element_type=F32)
        mixed = mixed + jnp.dot(s.wmat[k, 1], both_cols, preferred_element_type=F32)
        s.macc[0] += mixed[:, 0:128]
        s.macc[1] += mixed[:, 128:256]

    def at(step, lag, stage):
        @pl.when((step >= lag) & (step < lag + chunks))
        def _():
            stage(step - lag)

    @pl.loop(0, chunks + 5)
    def _(step):
        at(step, 0, arrive)
        at(step, 1, forward)
        at(step, 3, pass_on)
        at(step, 4, finish)
        at(step, 2, experts_of)
        at(step, 5, combine)

    mix_copy = remote(s.macc.at[oc], s.mix_r, s.one_ss.at[2], s.one_rs.at[2], partner)
    mix_copy.start()
    own = s.resid[...] + s.macc[mc]
    mix_copy.wait_recv()
    out_ref[...] = (own + s.mix_r[...]).astype(BF16)

    for copy in first_stats + second_stats + [gain_copy, resid_copy, mix_copy] + remote_w + halos:
        copy.wait_send()

    def left_q(q):
        send(q).wait_send()
        send_back(q).wait_send()

    @pl.loop(0, chunks)
    def _(k):
        per_block(k, left_q, lambda q: None)
        for copy in gather_copies(k):
            copy.wait_send()
        for way in range(2):
            for i in range(3):
                sum_copy(k, way, i).wait_send()


def shards(frames, conv_kernel, conv_gain, ffn_gain, lengths, routes, route_weights, w_gate, w_up, w_down):
    rows, width = frames.shape
    _, depth, hid = w_gate.shape
    scratch = names(rows, width, hid, depth, conv_kernel.shape[0])
    vmem = pl.BlockSpec(memory_space=pltpu.VMEM)
    return pl.pallas_call(
        functools.partial(kernel, tuple(scratch)),
        out_shape=jax.ShapeDtypeStruct((rows, width), BF16),
        in_specs=[pl.BlockSpec(memory_space=pltpu.SMEM)] + [vmem] * 6 + [pl.BlockSpec(memory_space=pl.ANY)] * 3,
        out_specs=vmem,
        scratch_shapes=list(scratch.values()),
        compiler_params=pltpu.CompilerParams(collective_id=0, has_side_effects=True, vmem_limit_bytes=56 * 1024 * 1024),
    )(
        lengths,
        frames,
        conv_kernel,
        conv_gain.reshape(1, width),
        ffn_gain.reshape(1, width),
        routes.T,
        route_weights.T,
        w_gate.reshape(depth, hid),
        w_up.reshape(depth, hid),
        w_down.reshape(hid, depth),
    )


def solution(mesh):
    in_specs = (
        P("tm", "tensor"),
        P(None, "tensor"),
        P("tensor"),
        P("tensor"),
        P(),
        P("tm", None),
        P("tm", None),
        P("tm", None, "tensor"),
        P("tm", None, "tensor"),
        P("tm", "tensor", None),
    )
    return jax.shard_map(shards, mesh=mesh, in_specs=in_specs, out_specs=P("tm", "tensor"), check_vma=False)
```

```python
import functools
import types

import jax
import jax.numpy as jnp
from jax import lax
from jax.experimental import pallas as pl
from jax.experimental.pallas import tpu as pltpu
from jax.sharding import PartitionSpec as P

MESH = pl.DeviceIdType.MESH
EPS = 1e-05
CAP = 24
NX = 4
NZ = 8
NY = 8
ORDER = (4, 3, 2, 0, 1, 7, 6, 5)
LAGS = (2, 6, 9, 12, 17)
F32 = jnp.float32
BF16 = jnp.bfloat16
I32 = jnp.int32


def div(a, b):
    return lax.div(a, jnp.int32(b))


def rem(a, b):
    return lax.rem(a, jnp.int32(b))


def remote(src, dst, ss, rs, dev):
    return pltpu.make_async_remote_copy(
        src_ref=src, dst_ref=dst, send_sem=ss, recv_sem=rs, device_id=dev, device_id_type=MESH
    )


def wait_all(ref, sem):
    pltpu.make_async_copy(ref, ref, sem).wait()


def spread(row):
    return jnp.broadcast_to(row, (128, 128)).T


def row_sums(value_ref, dst_ref, groups):
    for g in range(groups):
        v = value_ref[128 * g : 128 * (g + 1), :].astype(F32).T
        dst_ref[g : g + 1, :] = jnp.sum(v, axis=0, keepdims=True)
        dst_ref[groups + g : groups + g + 1, :] = jnp.sum(v * v, axis=0, keepdims=True)


def names(rows, width, hid, depth, taps, lens):
    groups = rows // 128
    chunks, per = NZ, NY // 2
    q = chunks * per
    crow = per * CAP
    hrow = crow // 2
    model = width * 2 * NX
    vm = pltpu.VMEM
    sem = pltpu.SemaphoreType.DMA
    return {
        "lens": pltpu.SMEM((lens,), I32),
        "frames": vm((rows, width), BF16),
        "taps": vm((taps, width), BF16),
        "cgain": vm((1, width), F32),
        "fgain": vm((1, width), F32),
        "routes": vm((2, rows), I32),
        "rw": vm((2, rows), F32),
        "in_sem": sem((7,)),
        "stat_s": vm((2, 2 * groups, 128), F32),
        "stat_r": vm((2, 2 * NX - 1, 2 * groups, 128), F32),
        "gain_s": vm((8, 128), F32),
        "gain_r": vm((8, 128), F32),
        "nbuf": vm((rows + 32, 128), F32),
        "edge_r": vm((2, 2 * NX, 2 * groups, 128), F32),
        "halo_r": vm((2, 16, 128), BF16),
        "behind": vm((rows, 128), I32),
        "ahead": vm((rows, 128), I32),
        "tapf": vm((32, 128), F32),
        "resid": vm((rows, 128), F32),
        "resid_p": vm((rows, 128), F32),
        "ein": vm((2, rows, 128), BF16),
        "pmat": vm((chunks, crow, rows), BF16),
        "dcol": vm((2, rows, 128), I32),
        "wcol": vm((2, rows, 128), F32),
        "wmat": vm((chunks, 2, rows, crow), BF16),
        "table": vm((q, 2 * CAP, 128), BF16),
        "gath": vm((NX, q, 2 * CAP, 128), BF16),
        "wg": vm((2, model, hid), BF16),
        "wu": vm((2, model, hid), BF16),
        "wd": vm((2, hid, model), BF16),
        "abuf": vm((crow, model), BF16),
        "hbuf": vm((crow, 2 * hid), BF16),
        "ybuf": vm((chunks, NX, crow, 256), F32),
        "rs_s": vm((chunks, 3, 2, hrow, 256), BF16),
        "rs_r": vm((chunks, 3, 2, hrow, 256), BF16),
        "back": vm((q, 2 * CAP, 128), BF16),
        "ret": vm((q, 2 * CAP, 128), BF16),
        "macc": vm((2, rows, 128), F32),
        "mix_r": vm((rows, 128), F32),
        "st_ss": sem((2,)),
        "st_rs": sem((2,)),
        "one_ss": sem((3,)),
        "one_rs": sem((3,)),
        "edge_ss": sem((2,)),
        "edge_rs": sem((2,)),
        "wl": sem((3,)),
        "w_ss": sem((3,)),
        "w_rs": sem((3,)),
        "a_ss": sem((1,)),
        "a_rs": sem((chunks,)),
        "g_ss": sem((1,)),
        "g_rs": sem((chunks, 2)),
        "r_ss": sem((1,)),
        "r_rs": sem((chunks, 2)),
        "b_ss": sem((1,)),
        "b_rs": sem((chunks,)),
    }


def kernel(keys, *refs):
    inputs, (wg_hbm, wu_hbm, wd_hbm, out_ref) = refs[:7], refs[7:11]
    s = types.SimpleNamespace(**dict(zip(keys, refs[11:])))
    frames_ref, taps_ref, cgain_ref, fgain_ref = s.frames, s.taps, s.cgain, s.fgain
    lengths_ref, routes_ref, rw_ref = s.lens, s.routes, s.rw
    brought = [
        pltpu.make_async_copy(src, dst, s.in_sem.at[i])
        for i, (src, dst) in enumerate(
            zip(inputs, (lengths_ref, frames_ref, taps_ref, cgain_ref, fgain_ref, routes_ref, rw_ref))
        )
    ]
    for i in (1, 0, 2, 3, 4, 5, 6):
        brought[i].start()
    rows, width = frames_ref.shape
    taps = taps_ref.shape[0]
    half = (taps - 1) // 2
    n_tm = NZ * NY
    n_t = 2 * NX
    model = width * n_t
    chunks = NZ
    per = NY // 2
    crow = per * CAP
    hrow = crow // 2
    groups = rows // 128

    tm = lax.axis_index("tm")
    ten = lax.axis_index("tensor")
    mz, my = div(tm, NY), rem(tm, NY)
    mx, mc = div(ten, 2), rem(ten, 2)
    oc = 1 - mc
    par = rem(my + mc, 2)
    own_q = ORDER.index(0) * per
    xr, xl, xo = rem(mx + 1, NX), rem(mx + NX - 1, NX), rem(mx + 2, NX)
    peer_t = mx * 2 + rem(my, 2)
    partner = (tm, mx * 2 + oc)
    right, left = (tm, xr * 2 + mc), (tm, xl * 2 + mc)
    sides = (rem(tm + n_tm - 1, n_tm), rem(tm + 1, n_tm))

    def offsets(q):
        k, i = div(q, per), rem(q, per)
        turn = jnp.int32(ORDER[0])
        for m in range(1, NZ):
            turn = turn + (ORDER[m] - ORDER[m - 1]) * div(k + NZ - m, NZ)
        return rem(2 * i + turn, NZ), 2 * i + par

    def dest(q):
        dz, dy = offsets(q)
        return (rem(mz + dz, NZ) * NY + rem(my + dy, NY), peer_t)

    def source(q):
        dz, dy = offsets(q)
        return (rem(mz + NZ - dz, NZ) * NY + rem(my + NY - dy, NY), peer_t)

    def tensor_peer(d):
        return (tm, rem(ten + d, n_t))

    bar = pltpu.get_barrier_semaphore()

    def greet(dev):
        pl.semaphore_signal(bar, inc=1, device_id=dev, device_id_type=MESH)

    for d in range(1, n_t):
        greet(tensor_peer(d))
    for side in sides:
        for d in range(n_t):
            greet((side, rem(ten + d, n_t)))

    @pl.loop(0, chunks * per)
    def _(q):
        @pl.when((q != own_q) | (par > 0))
        def _():
            greet(dest(q))

    hbm = (wg_hbm, wu_hbm, wd_hbm)
    wbuf = (s.wg, s.wu, s.wd)
    local_w = [pltpu.make_async_copy(hbm[i], wbuf[i].at[0], s.wl.at[i]) for i in range(3)]
    for copy in local_w:
        copy.start()
    brought[1].wait()
    row_sums(frames_ref, s.stat_s.at[0], groups)
    for i in (0, 2, 3, 4, 5, 6):
        brought[i].wait()
    s.gain_s[...] = jnp.broadcast_to(fgain_ref[...], (8, 128))
    pl.semaphore_wait(bar, n_t - 1 + 2 * n_t + chunks * per - 1 + par)

    def stat_copies(phase):
        return [
            remote(s.stat_s.at[phase], s.stat_r.at[phase, d - 1], s.st_ss.at[phase], s.st_rs.at[phase], tensor_peer(d))
            for d in range(1, n_t)
        ]

    def factors(tiles):
        total = tiles[0]
        for tile in tiles[1:]:
            total = total + tile
        mean = total[0:groups] / model
        square = total[groups : 2 * groups] / model
        return mean, lax.rsqrt(square - mean * mean + EPS)

    def norm_factors(phase):
        return factors([s.stat_s[phase]] + [s.stat_r[phase, d] for d in range(n_t - 1)])

    first_stats = stat_copies(0)
    halos = [
        remote(s.frames.at[pl.ds(i * (rows - 16), 16)], s.halo_r.at[1 - i], s.edge_ss.at[0], s.edge_rs.at[0], (sides[i], ten))
        for i in range(2)
    ]
    edges = [
        remote(s.stat_s.at[0], s.edge_r.at[1 - i, d], s.edge_ss.at[1], s.edge_rs.at[1], (sides[i], rem(ten + d, n_t)))
        for i in range(2)
        for d in range(n_t)
    ]
    for copy in first_stats + halos + edges:
        copy.start()
    gain_copy = remote(s.gain_s, s.gain_r, s.one_ss.at[0], s.one_rs.at[0], partner)
    gain_copy.start()
    remote_w = [remote(hbm[i], wbuf[i].at[1], s.w_ss.at[i], s.w_rs.at[i], partner) for i in range(3)]
    for copy in remote_w:
        copy.start()

    s.tapf[0:taps, :] = taps_ref[...].astype(F32)
    starts = [jnp.int32(0)]
    for i in range(lengths_ref.shape[0]):
        starts.append(starts[-1] + lengths_ref[i])

    @pl.loop(0, groups)
    def _(g):
        r0 = pl.multiple_of(g * 128, 128)
        pos = tm * rows + r0 + lax.broadcasted_iota(I32, (128, 128), 0)
        begin = jnp.zeros((128, 128), I32)
        end = jnp.full((128, 128), n_tm * rows, I32)
        for i in range(1, len(starts) - 1):
            begin = jnp.where(pos >= starts[i], starts[i], begin)
        for i in range(len(starts) - 2, 0, -1):
            end = jnp.where(pos < starts[i], starts[i], end)
        s.behind[pl.ds(r0, 128), :] = pos - begin
        s.ahead[pl.ds(r0, 128), :] = end - 1 - pos

    n_exp = n_tm
    names_k = [routes_ref[0:1, :], routes_ref[1:2, :]]
    experts = lax.broadcasted_iota(I32, (n_exp, rows), 0)
    hot = [experts == name for name in names_k]
    both = jnp.where(hot[0] | hot[1], 1.0, 0.0).astype(BF16)
    upper = jnp.where(
        lax.broadcasted_iota(I32, (rows, rows), 0) < lax.broadcasted_iota(I32, (rows, rows), 1), 1.0, 0.0
    ).astype(BF16)
    earlier = jnp.dot(both, upper, preferred_element_type=F32)
    target = []
    for k in range(2):
        slot = jnp.sum(jnp.where(hot[k], earlier, 0.0), axis=0, keepdims=True).astype(I32)
        ez, ey = names_k[k] >> 3, names_k[k] & 7
        dz = (ez - mz + NZ) & (NZ - 1)
        dy = (ey - my + NY) & (NY - 1)
        turn = jnp.zeros(dz.shape, I32)
        for m in range(1, NZ):
            turn = jnp.where(((dz - 2 * (dy >> 1)) & (NZ - 1)) == ORDER[m], m, turn)
        q = turn * per + (dy >> 1)
        target.append(jnp.where((dy & 1) == par, q * CAP + slot, -1))
    place = lax.broadcasted_iota(I32, (crow, rows), 0)

    @pl.loop(0, chunks)
    def _(k):
        here = place + k * crow
        s.pmat[k] = jnp.where((here == target[0]) | (here == target[1]), 1.0, 0.0).astype(BF16)

    wait_all(s.stat_r.at[0], s.st_rs.at[0])

    mean, scale = norm_factors(0)
    for g in range(groups):
        x = frames_ref[128 * g : 128 * (g + 1), :].astype(F32)
        n = ((x - spread(mean[g : g + 1])) * spread(scale[g : g + 1]) * cgain_ref[...]).astype(BF16)
        s.nbuf[16 + 128 * g : 16 + 128 * (g + 1), :] = n.astype(F32)
    block = 64

    def conv(r0):
        acc = jnp.zeros((block, 128), F32)
        back_n = s.behind[pl.ds(r0, block), :]
        ahead_n = s.ahead[pl.ds(r0, block), :]
        for j in range(taps):
            d = j - half
            term = s.nbuf[pl.ds(r0 + 16 + d, block), :] * s.tapf[j : j + 1, :]
            if d < 0:
                term = jnp.where(back_n >= -d, term, 0.0)
            if d > 0:
                term = jnp.where(ahead_n >= d, term, 0.0)
            acc = acc + term
        x = frames_ref[pl.ds(r0, block), :].astype(F32)
        s.resid[pl.ds(r0, block), :] = x + acc / (1.0 + jnp.exp(-acc))

    for r0 in range(block, rows - block, block):
        conv(r0)
    wait_all(s.halo_r, s.edge_rs.at[0])
    wait_all(s.edge_r, s.edge_rs.at[1])
    for i, g in enumerate((groups - 1, 0)):
        mean, scale = factors([s.edge_r[i, d] for d in range(n_t)])
        span = slice(112, 128) if i == 0 else slice(0, 16)
        x = s.halo_r[i].astype(F32)
        n = ((x - spread(mean[g : g + 1])[span]) * spread(scale[g : g + 1])[span] * cgain_ref[...]).astype(BF16)
        s.nbuf[i * (rows + 16) : i * (rows + 16) + 16, :] = n.astype(F32)
    conv(0)
    conv(rows - block)

    resid_copy = remote(s.resid, s.resid_p, s.one_ss.at[1], s.one_rs.at[1], partner)
    resid_copy.start()
    row_sums(s.resid, s.stat_s.at[1], groups)
    second_stats = stat_copies(1)
    for copy in second_stats:
        copy.start()

    for k in range(2):
        for g in range(groups):
            lanes = slice(128 * g, 128 * (g + 1))
            s.dcol[k, lanes, :] = spread(target[k][:, lanes].astype(F32)).astype(I32)
            s.wcol[k, lanes, :] = spread(rw_ref[k : k + 1, lanes])

    gain_copy.wait_recv()
    resid_copy.wait_recv()
    wait_all(s.stat_r.at[1], s.st_rs.at[1])
    mean, scale = norm_factors(1)
    for g in range(groups):
        m, r = spread(mean[g : g + 1]), spread(scale[g : g + 1])
        lanes = pl.ds(128 * g, 128)
        s.ein[mc, lanes, :] = ((s.resid[lanes, :] - m) * r * fgain_ref[...]).astype(BF16)
        s.ein[oc, lanes, :] = ((s.resid_p[lanes, :] - m) * r * s.gain_r[0:1, :]).astype(BF16)

    def send(q):
        return remote(s.table.at[q], s.gath.at[mx, q], s.a_ss.at[0], s.a_rs.at[div(q, per)], dest(q))

    def keep(q):
        return pltpu.make_async_copy(s.table.at[q], s.gath.at[mx, q], s.a_rs.at[div(q, per)])

    def pack(value):
        v = jnp.concatenate([value[:, 0:128].reshape(per, CAP, 128), value[:, 128:256].reshape(per, CAP, 128)], axis=1)
        return v.astype(BF16)

    def unpack(value):
        v = value.astype(F32)
        return v[:, :CAP, :].reshape(crow, 128).astype(BF16), v[:, CAP:, :].reshape(crow, 128).astype(BF16)

    def per_block(k, remotely, locally):
        @pl.loop(k * per, (k + 1) * per)
        def _(q):
            @pl.when((q != own_q) | (par > 0))
            def _():
                remotely(q)

            @pl.when((q == own_q) & (par == 0))
            def _():
                locally(q)

    def dispatch(k):
        both_cols = jnp.concatenate([s.ein[0], s.ein[1]], axis=1)
        picked = jnp.dot(s.pmat[k], both_cols, preferred_element_type=F32)
        s.table[pl.ds(k * per, per)] = pack(picked)
        per_block(k, lambda q: send(q).start(), lambda q: keep(q).start())

    @pl.loop(0, chunks)
    def _(k):
        dispatch(k)

    @pl.loop(0, chunks)
    def _(k):
        here = k * crow + lax.broadcasted_iota(I32, (128, crow), 1)
        for g in range(groups):
            lanes = slice(128 * g, 128 * (g + 1))
            w = jnp.where(here == s.dcol[0, lanes, 0:1], s.wcol[0, lanes, 0:1], 0.0)
            w = w + jnp.where(here == s.dcol[1, lanes, 0:1], s.wcol[1, lanes, 0:1], 0.0)
            high = w.astype(BF16)
            s.wmat[k, 0, lanes, :] = high
            s.wmat[k, 1, lanes, :] = (w - high.astype(F32)).astype(BF16)

    s.macc[...] = jnp.zeros(s.macc.shape, F32)

    def gather_copies(k):
        whole, first, second = pl.ds(k * per, per), pl.ds(k * per, per // 2), pl.ds(k * per + per // 2, per // 2)

        def along(x, span, i, dev):
            return remote(s.gath.at[x, span], s.gath.at[x, span], s.g_ss.at[0], s.g_rs.at[k, i // 2], dev)

        return (
            along(mx, whole, 0, right),
            along(mx, whole, 1, left),
            along(xl, first, 2, right),
            along(xr, second, 3, left),
        )

    def sum_copy(k, way, i):
        return remote(s.rs_s.at[k, i, way], s.rs_r.at[k, i, way], s.r_ss.at[0], s.r_rs.at[k, min(i, 1)], (right, left)[way])

    def send_back(q):
        return remote(s.back.at[q], s.ret.at[q], s.b_ss.at[0], s.b_rs.at[div(q, per)], source(q))

    def keep_back(q):
        return pltpu.make_async_copy(s.back.at[q], s.ret.at[q], s.b_rs.at[div(q, per)])

    for copy in local_w:
        copy.wait()
    for copy in remote_w:
        copy.wait_recv()

    def arrive(k):
        wait_all(s.gath.at[mx, pl.ds(k * per, per)], s.a_rs.at[k])
        to_right, to_left, _, _ = gather_copies(k)
        to_right.start()
        to_left.start()

    def forward(k):
        _, _, on_right, on_left = gather_copies(k)
        wait_all(s.gath.at[pl.ds(0, 2), pl.ds(k * per, per)], s.g_rs.at[k, 0])
        on_right.start()
        on_left.start()

    def experts_of(k):
        wait_all(s.gath.at[0, pl.ds(k * per, per)], s.g_rs.at[k, 1])
        for x in range(NX):
            low, high = unpack(s.gath[x, pl.ds(k * per, per)])
            s.abuf[:, 256 * x : 256 * x + 128] = low
            s.abuf[:, 256 * x + 128 : 256 * x + 256] = high
        hid = s.wg.shape[2]
        for c in range(2):
            for n in range(0, hid, 256):
                gate = jnp.dot(s.abuf[...], s.wg[c, :, n : n + 256], preferred_element_type=F32)
                up = jnp.dot(s.abuf[...], s.wu[c, :, n : n + 256], preferred_element_type=F32)
                s.hbuf[:, hid * c + n : hid * c + n + 256] = (gate / (1.0 + jnp.exp(-gate)) * up).astype(BF16)
        for n in range(NX):
            cols = slice(256 * n, 256 * (n + 1))
            y = jnp.dot(s.hbuf[:, :hid], s.wd[0, :, cols], preferred_element_type=F32)
            s.ybuf[k, n] = y + jnp.dot(s.hbuf[:, hid:], s.wd[1, :, cols], preferred_element_type=F32)
        s.rs_s[k, 0, 0] = s.ybuf[k, xo, 0:hrow, :].astype(BF16)
        sum_copy(k, 0, 0).start()
        s.rs_s[k, 0, 1] = s.ybuf[k, xo, hrow:crow, :].astype(BF16)
        sum_copy(k, 1, 0).start()
        s.rs_s[k, 1, 0] = s.ybuf[k, xr, hrow:crow, :].astype(BF16)
        sum_copy(k, 0, 1).start()
        s.rs_s[k, 1, 1] = s.ybuf[k, xl, 0:hrow, :].astype(BF16)
        sum_copy(k, 1, 1).start()

    def pass_on(k):
        wait_all(s.rs_r.at[k, 0], s.r_rs.at[k, 0])
        s.rs_s[k, 2, 0] = (s.ybuf[k, xr, 0:hrow, :] + s.rs_r[k, 0, 0].astype(F32)).astype(BF16)
        sum_copy(k, 0, 2).start()
        s.rs_s[k, 2, 1] = (s.ybuf[k, xl, hrow:crow, :] + s.rs_r[k, 0, 1].astype(F32)).astype(BF16)
        sum_copy(k, 1, 2).start()

    def finish(k):
        wait_all(s.rs_r.at[k, pl.ds(1, 2)], s.r_rs.at[k, 1])
        top = s.ybuf[k, mx, 0:hrow, :] + s.rs_r[k, 2, 0].astype(F32) + s.rs_r[k, 1, 1].astype(F32)
        low = s.ybuf[k, mx, hrow:crow, :] + s.rs_r[k, 2, 1].astype(F32) + s.rs_r[k, 1, 0].astype(F32)
        s.back[pl.ds(k * per, per)] = pack(jnp.concatenate([top, low], axis=0))
        per_block(k, lambda q: send_back(q).start(), lambda q: keep_back(q).start())

    def combine(k):
        wait_all(s.ret.at[pl.ds(k * per, per)], s.b_rs.at[k])
        low, high = unpack(s.ret[pl.ds(k * per, per)])
        both_cols = jnp.concatenate([low, high], axis=1)
        mixed = jnp.dot(s.wmat[k, 0], both_cols, preferred_element_type=F32)
        mixed = mixed + jnp.dot(s.wmat[k, 1], both_cols, preferred_element_type=F32)
        s.macc[0] += mixed[:, 0:128]
        s.macc[1] += mixed[:, 128:256]

    def at(step, lag, stage):
        @pl.when((step >= lag) & (step < lag + chunks))
        def _():
            stage(step - lag)

    @pl.loop(0, chunks + LAGS[4])
    def _(step):
        at(step, 0, arrive)
        at(step, LAGS[0], forward)
        at(step, LAGS[2], pass_on)
        at(step, LAGS[3], finish)
        at(step, LAGS[1], experts_of)
        at(step, LAGS[4], combine)

    mix_copy = remote(s.macc.at[oc], s.mix_r, s.one_ss.at[2], s.one_rs.at[2], partner)
    mix_copy.start()
    own = s.resid[...] + s.macc[mc]
    mix_copy.wait_recv()
    out_ref[...] = (own + s.mix_r[...]).astype(BF16)

    for copy in [gain_copy, resid_copy, mix_copy] + remote_w:
        copy.wait_send()
    for phase in range(2):
        wait_all(s.stat_r.at[phase], s.st_ss.at[phase])
    wait_all(s.halo_r, s.edge_ss.at[0])
    wait_all(s.edge_r, s.edge_ss.at[1])
    wait_all(s.gath.at[pl.ds(0, 3)], s.g_ss.at[0])
    wait_all(s.rs_s, s.r_ss.at[0])
    others = chunks * per - 1
    wait_all(s.table.at[pl.ds(0, others)], s.a_ss.at[0])
    wait_all(s.back.at[pl.ds(0, others)], s.b_ss.at[0])

    @pl.when(par > 0)
    def _():
        wait_all(s.table.at[0], s.a_ss.at[0])
        wait_all(s.back.at[0], s.b_ss.at[0])


def shards(frames, conv_kernel, conv_gain, ffn_gain, lengths, routes, route_weights, w_gate, w_up, w_down):
    rows, width = frames.shape
    _, depth, hid = w_gate.shape
    scratch = names(rows, width, hid, depth, conv_kernel.shape[0], lengths.shape[0])
    vmem = pl.BlockSpec(memory_space=pltpu.VMEM)
    return pl.pallas_call(
        functools.partial(kernel, tuple(scratch)),
        out_shape=jax.ShapeDtypeStruct((rows, width), BF16),
        in_specs=[pl.BlockSpec(memory_space=pl.ANY)] * 10,
        out_specs=vmem,
        scratch_shapes=list(scratch.values()),
        compiler_params=pltpu.CompilerParams(collective_id=0, has_side_effects=True, vmem_limit_bytes=56 * 1024 * 1024),
    )(
        lengths,
        frames,
        conv_kernel,
        conv_gain.reshape(1, width),
        ffn_gain.reshape(1, width),
        routes.T,
        route_weights.T,
        w_gate.reshape(depth, hid),
        w_up.reshape(depth, hid),
        w_down.reshape(hid, depth),
    )


def solution(mesh):
    in_specs = (
        P("tm", "tensor"),
        P(None, "tensor"),
        P("tensor"),
        P("tensor"),
        P(),
        P("tm", None),
        P("tm", None),
        P("tm", None, "tensor"),
        P("tm", None, "tensor"),
        P("tm", "tensor", None),
    )
    return jax.shard_map(shards, mesh=mesh, in_specs=in_specs, out_specs=P("tm", "tensor"), check_vma=False)
```

```python
import functools
import types

import jax
import jax.numpy as jnp
from jax import lax
from jax.experimental import pallas as pl
from jax.experimental.pallas import tpu as pltpu
from jax.sharding import PartitionSpec as P

MESH = pl.DeviceIdType.MESH
EPS = 1e-05
CAP = 24
NX = 4
NZ = 8
NY = 8
ORDER = (6, 5, 2, 1, 0, 7, 3, 4)
EARLY = 2
SEND_EARLY = 3
LAGS = (2, 5, 8, 11, 16)
F32 = jnp.float32
BF16 = jnp.bfloat16
I32 = jnp.int32


def div(a, b):
    return lax.div(a, jnp.int32(b))


def rem(a, b):
    return lax.rem(a, jnp.int32(b))


def remote(src, dst, ss, rs, dev):
    return pltpu.make_async_remote_copy(
        src_ref=src, dst_ref=dst, send_sem=ss, recv_sem=rs, device_id=dev, device_id_type=MESH
    )


def wait_all(ref, sem):
    pltpu.make_async_copy(ref, ref, sem).wait()


def spread(row):
    return jnp.broadcast_to(row, (128, 128)).T


def row_sums(value_ref, dst_ref, groups):
    for g in range(groups):
        v = value_ref[128 * g : 128 * (g + 1), :].astype(F32).T
        dst_ref[g : g + 1, :] = jnp.sum(v, axis=0, keepdims=True)
        dst_ref[groups + g : groups + g + 1, :] = jnp.sum(v * v, axis=0, keepdims=True)


def names(rows, width, hid, depth, taps, lens):
    groups = rows // 128
    chunks, per = NZ, NY // 2
    q = chunks * per
    crow = per * CAP
    hrow = crow // 2
    model = width * 2 * NX
    vm = pltpu.VMEM
    sem = pltpu.SemaphoreType.DMA
    return {
        "lens": pltpu.SMEM((lens,), I32),
        "frames": vm((rows, width), BF16),
        "taps": vm((taps, width), BF16),
        "cgain": vm((1, width), F32),
        "fgain": vm((1, width), F32),
        "routes": vm((2, rows), I32),
        "rw": vm((2, rows), F32),
        "in_sem": sem((7,)),
        "stat_s": vm((2, 2 * groups, 128), F32),
        "stat_r": vm((2, 2 * NX - 1, 2 * groups, 128), F32),
        "gain_s": vm((8, 128), F32),
        "gain_r": vm((8, 128), F32),
        "nbuf": vm((rows + 32, 128), F32),
        "edge_r": vm((2, 2 * NX, 2 * groups, 128), F32),
        "halo_r": vm((2, 16, 128), BF16),
        "behind": vm((rows, 128), I32),
        "ahead": vm((rows, 128), I32),
        "tapf": vm((32, 128), F32),
        "resid": vm((rows, 128), F32),
        "resid_p": vm((rows, 128), F32),
        "ein": vm((2, rows, 128), BF16),
        "pmat": vm((chunks, crow, rows), BF16),
        "dcol": vm((2, rows, 128), I32),
        "wcol": vm((2, rows, 128), F32),
        "wmat": vm((chunks, 2, rows, crow), BF16),
        "table": vm((q - EARLY * per, 2 * CAP, 128), BF16),
        "pre": vm((NX, EARLY * per, 2 * CAP, 128), BF16),
        "gath": vm((NX, q, 2 * CAP, 128), BF16),
        "wg": vm((2, model, hid), BF16),
        "wu": vm((2, model, hid), BF16),
        "wd": vm((2, hid, model), BF16),
        "abuf": vm((crow, model), BF16),
        "hbuf": vm((crow, 2 * hid), BF16),
        "ybuf": vm((chunks, NX, crow, 256), F32),
        "rs_s": vm((chunks, 3, 2, hrow, 256), BF16),
        "rs_r": vm((chunks, 3, 2, hrow, 256), BF16),
        "back": vm((q, 2 * CAP, 128), BF16),
        "ret": vm((q, 2 * CAP, 128), BF16),
        "macc": vm((2, rows, 128), F32),
        "mix_r": vm((rows, 128), F32),
        "st_ss": sem((2,)),
        "st_rs": sem((2,)),
        "one_ss": sem((3,)),
        "one_rs": sem((3,)),
        "edge_ss": sem((2,)),
        "edge_rs": sem((2,)),
        "wl": sem((3,)),
        "w_ss": sem((3,)),
        "w_rs": sem((3,)),
        "p_ss": sem((1,)),
        "p_rs": sem((2,)),
        "a_ss": sem((2,)),
        "a_rs": sem((chunks,)),
        "g_ss": sem((1,)),
        "g_rs": sem((chunks - EARLY, 2)),
        "r_ss": sem((1,)),
        "r_rs": sem((chunks, 2)),
        "b_ss": sem((1,)),
        "b_rs": sem((chunks,)),
    }


def kernel(keys, *refs):
    inputs, (wg_hbm, wu_hbm, wd_hbm, out_ref) = refs[:7], refs[7:11]
    s = types.SimpleNamespace(**dict(zip(keys, refs[11:])))
    frames_ref, taps_ref, cgain_ref, fgain_ref = s.frames, s.taps, s.cgain, s.fgain
    lengths_ref, routes_ref, rw_ref = s.lens, s.routes, s.rw
    brought = [
        pltpu.make_async_copy(src, dst, s.in_sem.at[i])
        for i, (src, dst) in enumerate(
            zip(inputs, (lengths_ref, frames_ref, taps_ref, cgain_ref, fgain_ref, routes_ref, rw_ref))
        )
    ]
    for i in (1, 0, 2, 3, 4, 5, 6):
        brought[i].start()
    rows, width = frames_ref.shape
    taps = taps_ref.shape[0]
    half = (taps - 1) // 2
    n_tm = NZ * NY
    n_t = 2 * NX
    model = width * n_t
    chunks = NZ
    per = NY // 2
    crow = per * CAP
    hrow = crow // 2
    groups = rows // 128

    tm = lax.axis_index("tm")
    ten = lax.axis_index("tensor")
    mz, my = div(tm, NY), rem(tm, NY)
    mx, mc = div(ten, 2), rem(ten, 2)
    oc = 1 - mc
    par = rem(my + mc, 2)
    own_k = ORDER.index(0)
    late = chunks - EARLY
    xr, xl, xo = rem(mx + 1, NX), rem(mx + NX - 1, NX), rem(mx + 2, NX)
    peer_t = mx * 2 + rem(my, 2)
    partner = (tm, mx * 2 + oc)
    right, left = (tm, xr * 2 + mc), (tm, xl * 2 + mc)
    sides = (rem(tm + n_tm - 1, n_tm), rem(tm + 1, n_tm))

    def turn_of(k):
        turn = jnp.int32(ORDER[0])
        for m in range(1, NZ):
            turn = turn + (ORDER[m] - ORDER[m - 1]) * div(k + NZ - m, NZ)
        return turn

    def dest(turn, i):
        return (rem(mz + 2 * i + turn, NZ) * NY + rem(my + 2 * i + par, NY), peer_t)

    def source(turn, i):
        return (rem(mz + 2 * NZ - 2 * i - turn, NZ) * NY + rem(my + 2 * NY - 2 * i - par, NY), peer_t)

    def per_block(k, remotely, locally=None):
        turn = turn_of(k)
        for i in range(per):
            if i > 0:
                remotely(k, turn, i)
                continue

            @pl.when((k != own_k) | (par > 0))
            def _():
                remotely(k, turn, 0)

            if locally is not None:

                @pl.when((k == own_k) & (par == 0))
                def _():
                    locally(k)

    def tensor_peer(d):
        return (tm, rem(ten + d, n_t))

    bar = pltpu.get_barrier_semaphore()

    def greet(dev):
        pl.semaphore_signal(bar, inc=1, device_id=dev, device_id_type=MESH)

    for d in range(1, n_t):
        greet(tensor_peer(d))
    for side in sides:
        for d in range(n_t):
            greet((side, rem(ten + d, n_t)))

    @pl.loop(0, chunks)
    def _(k):
        per_block(k, lambda k, turn, i: greet(dest(turn, i)))

    hbm = (wg_hbm, wu_hbm, wd_hbm)
    wbuf = (s.wg, s.wu, s.wd)
    local_w = [pltpu.make_async_copy(hbm[i], wbuf[i].at[0], s.wl.at[i]) for i in range(3)]
    for copy in local_w:
        copy.start()
    brought[1].wait()
    row_sums(frames_ref, s.stat_s.at[0], groups)
    for i in (0, 2, 3, 4, 5, 6):
        brought[i].wait()
    s.gain_s[...] = jnp.broadcast_to(fgain_ref[...], (8, 128))
    pl.semaphore_wait(bar, n_t - 1 + 2 * n_t + chunks * per - 1 + par)

    def stat_copies(phase):
        return [
            remote(s.stat_s.at[phase], s.stat_r.at[phase, d - 1], s.st_ss.at[phase], s.st_rs.at[phase], tensor_peer(d))
            for d in range(1, n_t)
        ]

    def factors(tiles):
        total = tiles[0]
        for tile in tiles[1:]:
            total = total + tile
        mean = total[0:groups] / model
        square = total[groups : 2 * groups] / model
        return mean, lax.rsqrt(square - mean * mean + EPS)

    def norm_factors(phase):
        return factors([s.stat_s[phase]] + [s.stat_r[phase, d] for d in range(n_t - 1)])

    first_stats = stat_copies(0)
    halos = [
        remote(s.frames.at[pl.ds(i * (rows - 16), 16)], s.halo_r.at[1 - i], s.edge_ss.at[0], s.edge_rs.at[0], (sides[i], ten))
        for i in range(2)
    ]
    edges = [
        remote(s.stat_s.at[0], s.edge_r.at[1 - i, d], s.edge_ss.at[1], s.edge_rs.at[1], (sides[i], rem(ten + d, n_t)))
        for i in range(2)
        for d in range(n_t)
    ]
    for copy in first_stats + halos + edges:
        copy.start()
    gain_copy = remote(s.gain_s, s.gain_r, s.one_ss.at[0], s.one_rs.at[0], partner)
    gain_copy.start()
    remote_w = [remote(hbm[i], wbuf[i].at[1], s.w_ss.at[i], s.w_rs.at[i], partner) for i in range(3)]
    for copy in remote_w:
        copy.start()

    s.tapf[0:taps, :] = taps_ref[...].astype(F32)
    starts = [jnp.int32(0)]
    for i in range(lengths_ref.shape[0]):
        starts.append(starts[-1] + lengths_ref[i])

    @pl.loop(0, groups)
    def _(g):
        r0 = pl.multiple_of(g * 128, 128)
        pos = tm * rows + r0 + lax.broadcasted_iota(I32, (128, 128), 0)
        begin = jnp.zeros((128, 128), I32)
        end = jnp.full((128, 128), n_tm * rows, I32)
        for i in range(1, len(starts) - 1):
            begin = jnp.where(pos >= starts[i], starts[i], begin)
        for i in range(len(starts) - 2, 0, -1):
            end = jnp.where(pos < starts[i], starts[i], end)
        s.behind[pl.ds(r0, 128), :] = pos - begin
        s.ahead[pl.ds(r0, 128), :] = end - 1 - pos

    n_exp = n_tm
    names_k = [routes_ref[0:1, :], routes_ref[1:2, :]]
    experts = lax.broadcasted_iota(I32, (n_exp, rows), 0)
    hot = [experts == name for name in names_k]
    both = jnp.where(hot[0] | hot[1], 1.0, 0.0).astype(BF16)
    upper = jnp.where(
        lax.broadcasted_iota(I32, (rows, rows), 0) < lax.broadcasted_iota(I32, (rows, rows), 1), 1.0, 0.0
    ).astype(BF16)
    earlier = jnp.dot(both, upper, preferred_element_type=F32)
    target = []
    for k in range(2):
        slot = jnp.sum(jnp.where(hot[k], earlier, 0.0), axis=0, keepdims=True).astype(I32)
        ez, ey = names_k[k] >> 3, names_k[k] & 7
        dz = (ez - mz + NZ) & (NZ - 1)
        dy = (ey - my + NY) & (NY - 1)
        turn = jnp.zeros(dz.shape, I32)
        for m in range(1, NZ):
            turn = jnp.where(((dz - 2 * (dy >> 1)) & (NZ - 1)) == ORDER[m], m, turn)
        q = turn * per + (dy >> 1)
        target.append(jnp.where((dy & 1) == par, q * CAP + slot, -1))
    place = lax.broadcasted_iota(I32, (crow, rows), 0)

    @pl.loop(0, chunks)
    def _(k):
        here = place + k * crow
        s.pmat[k] = jnp.where((here == target[0]) | (here == target[1]), 1.0, 0.0).astype(BF16)

    wait_all(s.stat_r.at[0], s.st_rs.at[0])

    mean, scale = norm_factors(0)
    for g in range(groups):
        x = frames_ref[128 * g : 128 * (g + 1), :].astype(F32)
        n = ((x - spread(mean[g : g + 1])) * spread(scale[g : g + 1]) * cgain_ref[...]).astype(BF16)
        s.nbuf[16 + 128 * g : 16 + 128 * (g + 1), :] = n.astype(F32)
    block = 64

    def conv(r0):
        acc = jnp.zeros((block, 128), F32)
        back_n = s.behind[pl.ds(r0, block), :]
        ahead_n = s.ahead[pl.ds(r0, block), :]
        for j in range(taps):
            d = j - half
            term = s.nbuf[pl.ds(r0 + 16 + d, block), :] * s.tapf[j : j + 1, :]
            if d < 0:
                term = jnp.where(back_n >= -d, term, 0.0)
            if d > 0:
                term = jnp.where(ahead_n >= d, term, 0.0)
            acc = acc + term
        x = frames_ref[pl.ds(r0, block), :].astype(F32)
        s.resid[pl.ds(r0, block), :] = x + acc / (1.0 + jnp.exp(-acc))

    for r0 in range(block, rows - block, block):
        conv(r0)
    wait_all(s.halo_r, s.edge_rs.at[0])
    wait_all(s.edge_r, s.edge_rs.at[1])
    for i, g in enumerate((groups - 1, 0)):
        mean, scale = factors([s.edge_r[i, d] for d in range(n_t)])
        span = slice(112, 128) if i == 0 else slice(0, 16)
        x = s.halo_r[i].astype(F32)
        n = ((x - spread(mean[g : g + 1])[span]) * spread(scale[g : g + 1])[span] * cgain_ref[...]).astype(BF16)
        s.nbuf[i * (rows + 16) : i * (rows + 16) + 16, :] = n.astype(F32)
    conv(0)
    conv(rows - block)

    resid_copy = remote(s.resid, s.resid_p, s.one_ss.at[1], s.one_rs.at[1], partner)
    resid_copy.start()
    row_sums(s.resid, s.stat_s.at[1], groups)
    second_stats = stat_copies(1)
    for copy in second_stats:
        copy.start()

    for k in range(2):
        for g in range(groups):
            lanes = slice(128 * g, 128 * (g + 1))
            s.dcol[k, lanes, :] = spread(target[k][:, lanes].astype(F32)).astype(I32)
            s.wcol[k, lanes, :] = spread(rw_ref[k : k + 1, lanes])

    gain_copy.wait_recv()
    resid_copy.wait_recv()
    wait_all(s.stat_r.at[1], s.st_rs.at[1])
    mean, scale = norm_factors(1)
    for g in range(groups):
        m, r = spread(mean[g : g + 1]), spread(scale[g : g + 1])
        lanes = pl.ds(128 * g, 128)
        s.ein[mc, lanes, :] = ((s.resid[lanes, :] - m) * r * fgain_ref[...]).astype(BF16)
        s.ein[oc, lanes, :] = ((s.resid_p[lanes, :] - m) * r * s.gain_r[0:1, :]).astype(BF16)

    def send(k, turn, i):
        q = k * per + i
        remote(s.table.at[q], s.gath.at[mx, q], s.a_ss.at[0], s.a_rs.at[k], dest(turn, i)).start()

    def keep(k):
        pltpu.make_async_copy(s.table.at[k * per], s.gath.at[mx, k * per], s.a_rs.at[k]).start()

    def pack(value):
        v = jnp.concatenate([value[:, 0:128].reshape(per, CAP, 128), value[:, 128:256].reshape(per, CAP, 128)], axis=1)
        return v.astype(BF16)

    def unpack(value):
        v = value.astype(F32)
        return v[:, :CAP, :].reshape(crow, 128).astype(BF16), v[:, CAP:, :].reshape(crow, 128).astype(BF16)

    def picked(k):
        both_cols = jnp.concatenate([s.ein[0], s.ein[1]], axis=1)
        return pack(jnp.dot(s.pmat[k], both_cols, preferred_element_type=F32))

    def early_copy(x, span, i, dev):
        return remote(s.pre.at[x, span], s.pre.at[x, span], s.p_ss.at[0], s.p_rs.at[i], dev)

    def send_early(k, turn, i):
        q = k * per + i
        remote(s.pre.at[:, q - late * per], s.gath.at[:, q], s.a_ss.at[1], s.a_rs.at[k], dest(turn, i)).start()

    @pl.loop(late, chunks)
    def _(k):
        s.pre[mx, pl.ds((k - late) * per, per)] = picked(k)

    n_early = EARLY * per
    early_copy(mx, pl.ds(0, n_early), 0, right).start()
    early_copy(mx, pl.ds(0, n_early), 0, left).start()

    def dispatch(k):
        s.table[pl.ds(k * per, per)] = picked(k)
        per_block(k, send, keep)

    @pl.loop(0, late)
    def _(k):
        dispatch(k)

    @pl.loop(0, chunks)
    def _(k):
        here = k * crow + lax.broadcasted_iota(I32, (128, crow), 1)
        for g in range(groups):
            lanes = slice(128 * g, 128 * (g + 1))
            w = jnp.where(here == s.dcol[0, lanes, 0:1], s.wcol[0, lanes, 0:1], 0.0)
            w = w + jnp.where(here == s.dcol[1, lanes, 0:1], s.wcol[1, lanes, 0:1], 0.0)
            high = w.astype(BF16)
            s.wmat[k, 0, lanes, :] = high
            s.wmat[k, 1, lanes, :] = (w - high.astype(F32)).astype(BF16)

    s.macc[...] = jnp.zeros(s.macc.shape, F32)

    def gather_copies(k):
        whole, first, second = pl.ds(k * per, per), pl.ds(k * per, per // 2), pl.ds(k * per + per // 2, per // 2)

        def along(x, span, i, dev):
            return remote(s.gath.at[x, span], s.gath.at[x, span], s.g_ss.at[0], s.g_rs.at[k, i // 2], dev)

        return (
            along(mx, whole, 0, right),
            along(mx, whole, 1, left),
            along(xl, first, 2, right),
            along(xr, second, 3, left),
        )

    def sum_copy(k, way, i):
        return remote(s.rs_s.at[k, i, way], s.rs_r.at[k, i, way], s.r_ss.at[0], s.r_rs.at[k, min(i, 1)], (right, left)[way])

    def send_back(k, turn, i):
        q = k * per + i
        remote(s.back.at[q], s.ret.at[q], s.b_ss.at[0], s.b_rs.at[k], source(turn, i)).start()

    def keep_back(k):
        pltpu.make_async_copy(s.back.at[k * per], s.ret.at[k * per], s.b_rs.at[k]).start()

    for copy in local_w:
        copy.wait()
    for copy in remote_w:
        copy.wait_recv()

    def leave_early():
        wait_all(s.pre.at[0], s.p_rs.at[1])

        @pl.loop(late, chunks)
        def _(k):
            per_block(k, send_early)

    def arrive(k):
        wait_all(s.gath.at[mx, pl.ds(k * per, per)], s.a_rs.at[k])
        to_right, to_left, _, _ = gather_copies(k)
        to_right.start()
        to_left.start()

    def forward(k):
        _, _, on_right, on_left = gather_copies(k)
        wait_all(s.gath.at[pl.ds(0, 2), pl.ds(k * per, per)], s.g_rs.at[k, 0])
        on_right.start()
        on_left.start()

    def experts_of(k):
        @pl.when(k < late)
        def _():
            wait_all(s.gath.at[0, pl.ds(k * per, per)], s.g_rs.at[k, 1])

        @pl.when(k >= late)
        def _():
            wait_all(s.gath.at[:, pl.ds(k * per, per)], s.a_rs.at[k])

        for x in range(NX):
            low, high = unpack(s.gath[x, pl.ds(k * per, per)])
            s.abuf[:, 256 * x : 256 * x + 128] = low
            s.abuf[:, 256 * x + 128 : 256 * x + 256] = high
        hid = s.wg.shape[2]
        for c in range(2):
            for n in range(0, hid, 256):
                gate = jnp.dot(s.abuf[...], s.wg[c, :, n : n + 256], preferred_element_type=F32)
                up = jnp.dot(s.abuf[...], s.wu[c, :, n : n + 256], preferred_element_type=F32)
                s.hbuf[:, hid * c + n : hid * c + n + 256] = (gate / (1.0 + jnp.exp(-gate)) * up).astype(BF16)
        for n in range(NX):
            cols = slice(256 * n, 256 * (n + 1))
            y = jnp.dot(s.hbuf[:, :hid], s.wd[0, :, cols], preferred_element_type=F32)
            s.ybuf[k, n] = y + jnp.dot(s.hbuf[:, hid:], s.wd[1, :, cols], preferred_element_type=F32)
        s.rs_s[k, 0, 0] = s.ybuf[k, xo, 0:hrow, :].astype(BF16)
        sum_copy(k, 0, 0).start()
        s.rs_s[k, 0, 1] = s.ybuf[k, xo, hrow:crow, :].astype(BF16)
        sum_copy(k, 1, 0).start()
        s.rs_s[k, 1, 0] = s.ybuf[k, xr, hrow:crow, :].astype(BF16)
        sum_copy(k, 0, 1).start()
        s.rs_s[k, 1, 1] = s.ybuf[k, xl, 0:hrow, :].astype(BF16)
        sum_copy(k, 1, 1).start()

    def pass_on(k):
        wait_all(s.rs_r.at[k, 0], s.r_rs.at[k, 0])
        s.rs_s[k, 2, 0] = (s.ybuf[k, xr, 0:hrow, :] + s.rs_r[k, 0, 0].astype(F32)).astype(BF16)
        sum_copy(k, 0, 2).start()
        s.rs_s[k, 2, 1] = (s.ybuf[k, xl, hrow:crow, :] + s.rs_r[k, 0, 1].astype(F32)).astype(BF16)
        sum_copy(k, 1, 2).start()

    def finish(k):
        wait_all(s.rs_r.at[k, pl.ds(1, 2)], s.r_rs.at[k, 1])
        top = s.ybuf[k, mx, 0:hrow, :] + s.rs_r[k, 2, 0].astype(F32) + s.rs_r[k, 1, 1].astype(F32)
        low = s.ybuf[k, mx, hrow:crow, :] + s.rs_r[k, 2, 1].astype(F32) + s.rs_r[k, 1, 0].astype(F32)
        s.back[pl.ds(k * per, per)] = pack(jnp.concatenate([top, low], axis=0))
        per_block(k, send_back, keep_back)

    def combine(k):
        wait_all(s.ret.at[pl.ds(k * per, per)], s.b_rs.at[k])
        low, high = unpack(s.ret[pl.ds(k * per, per)])
        both_cols = jnp.concatenate([low, high], axis=1)
        mixed = jnp.dot(s.wmat[k, 0], both_cols, preferred_element_type=F32)
        mixed = mixed + jnp.dot(s.wmat[k, 1], both_cols, preferred_element_type=F32)
        s.macc[0] += mixed[:, 0:128]
        s.macc[1] += mixed[:, 128:256]

    def at(step, lag, stage, count=chunks):
        @pl.when((step >= lag) & (step < lag + count))
        def _():
            stage(step - lag)

    wait_all(s.pre.at[pl.ds(0, 2)], s.p_rs.at[0])
    early_copy(xl, pl.ds(0, n_early // 2), 1, right).start()
    early_copy(xr, pl.ds(n_early // 2, n_early // 2), 1, left).start()

    @pl.loop(0, chunks + LAGS[4])
    def _(step):
        pl.when(step == SEND_EARLY)(leave_early)
        at(step, 0, arrive, late)
        at(step, LAGS[0], forward, late)
        at(step, LAGS[2], pass_on)
        at(step, LAGS[3], finish)
        at(step, LAGS[1], experts_of)
        at(step, LAGS[4], combine)

    mix_copy = remote(s.macc.at[oc], s.mix_r, s.one_ss.at[2], s.one_rs.at[2], partner)
    mix_copy.start()
    own = s.resid[...] + s.macc[mc]
    mix_copy.wait_recv()
    out_ref[...] = (own + s.mix_r[...]).astype(BF16)

    for copy in [gain_copy, resid_copy, mix_copy] + remote_w:
        copy.wait_send()
    for phase in range(2):
        wait_all(s.stat_r.at[phase], s.st_ss.at[phase])
    wait_all(s.halo_r, s.edge_ss.at[0])
    wait_all(s.edge_r, s.edge_ss.at[1])
    wait_all(s.gath.at[pl.ds(0, 3), pl.ds(0, late * per)], s.g_ss.at[0])
    wait_all(s.pre.at[pl.ds(0, 3)], s.p_ss.at[0])
    wait_all(s.pre, s.a_ss.at[1])
    wait_all(s.rs_s, s.r_ss.at[0])
    wait_all(s.table.at[pl.ds(0, late * per - 1)], s.a_ss.at[0])
    wait_all(s.back.at[pl.ds(0, chunks * per - 1)], s.b_ss.at[0])

    @pl.when(par > 0)
    def _():
        wait_all(s.table.at[0], s.a_ss.at[0])
        wait_all(s.back.at[0], s.b_ss.at[0])


def shards(frames, conv_kernel, conv_gain, ffn_gain, lengths, routes, route_weights, w_gate, w_up, w_down):
    rows, width = frames.shape
    _, depth, hid = w_gate.shape
    scratch = names(rows, width, hid, depth, conv_kernel.shape[0], lengths.shape[0])
    vmem = pl.BlockSpec(memory_space=pltpu.VMEM)
    return pl.pallas_call(
        functools.partial(kernel, tuple(scratch)),
        out_shape=jax.ShapeDtypeStruct((rows, width), BF16),
        in_specs=[pl.BlockSpec(memory_space=pl.ANY)] * 10,
        out_specs=vmem,
        scratch_shapes=list(scratch.values()),
        compiler_params=pltpu.CompilerParams(collective_id=0, has_side_effects=True, vmem_limit_bytes=56 * 1024 * 1024),
    )(
        lengths,
        frames,
        conv_kernel,
        conv_gain.reshape(1, width),
        ffn_gain.reshape(1, width),
        routes.T,
        route_weights.T,
        w_gate.reshape(depth, hid),
        w_up.reshape(depth, hid),
        w_down.reshape(hid, depth),
    )


def solution(mesh):
    in_specs = (
        P("tm", "tensor"),
        P(None, "tensor"),
        P("tensor"),
        P("tensor"),
        P(),
        P("tm", None),
        P("tm", None),
        P("tm", None, "tensor"),
        P("tm", None, "tensor"),
        P("tm", "tensor", None),
    )
    return jax.shard_map(shards, mesh=mesh, in_specs=in_specs, out_specs=P("tm", "tensor"), check_vma=False)
```

```python
import functools
import types

import jax
import jax.numpy as jnp
from jax import lax
from jax.experimental import pallas as pl
from jax.experimental.pallas import tpu as pltpu
from jax.sharding import PartitionSpec as P

MESH = pl.DeviceIdType.MESH
EPS = 1e-05
CAP = 24
NX = 4
NZ = 8
NY = 8
ORDER = (0, 7, 1, 3, 5, 2, 6, 4)
EARLY = 2
SEND_EARLY = 2
LAGS = (3, 6, 9, 12, 21)
F32 = jnp.float32
BF16 = jnp.bfloat16
I32 = jnp.int32


def div(a, b):
    return lax.div(a, jnp.int32(b))


def rem(a, b):
    return lax.rem(a, jnp.int32(b))


def remote(src, dst, ss, rs, dev):
    return pltpu.make_async_remote_copy(
        src_ref=src, dst_ref=dst, send_sem=ss, recv_sem=rs, device_id=dev, device_id_type=MESH
    )


def wait_all(ref, sem):
    pltpu.make_async_copy(ref, ref, sem).wait()


def spread(row):
    return jnp.broadcast_to(row, (128, 128)).T


def row_sums(value_ref, dst_ref, groups):
    for g in range(groups):
        v = value_ref[128 * g : 128 * (g + 1), :].astype(F32).T
        dst_ref[g : g + 1, :] = jnp.sum(v, axis=0, keepdims=True)
        dst_ref[groups + g : groups + g + 1, :] = jnp.sum(v * v, axis=0, keepdims=True)


def names(rows, width, hid, depth, taps, lens):
    groups = rows // 128
    chunks, per = NZ, NY // 2
    q = chunks * per
    crow = per * CAP
    hrow = crow // 2
    model = width * 2 * NX
    vm = pltpu.VMEM
    sem = pltpu.SemaphoreType.DMA
    return {
        "lens": pltpu.SMEM((lens,), I32),
        "frames": vm((rows, width), BF16),
        "taps": vm((taps, width), BF16),
        "cgain": vm((1, width), F32),
        "fgain": vm((1, width), F32),
        "routes": vm((2, rows), I32),
        "rw": vm((2, rows), F32),
        "in_sem": sem((7,)),
        "stat_s": vm((2, 2 * groups, 128), F32),
        "stat_r": vm((2, 2 * NX - 1, 2 * groups, 128), F32),
        "gain_s": vm((8, 128), F32),
        "gain_r": vm((8, 128), F32),
        "nbuf": vm((rows + 32, 128), F32),
        "edge_r": vm((2, 2 * NX, 2 * groups, 128), F32),
        "halo_r": vm((2, 16, 128), BF16),
        "behind": vm((rows, 128), I32),
        "ahead": vm((rows, 128), I32),
        "tapf": vm((32, 128), F32),
        "resid": vm((rows, 128), F32),
        "resid_p": vm((rows, 128), F32),
        "ein": vm((2, rows, 128), BF16),
        "pmat": vm((chunks, crow, rows), BF16),
        "dcol": vm((2, rows, 128), I32),
        "wcol": vm((2, rows, 128), F32),
        "wmat": vm((chunks, 2, rows, crow), BF16),
        "table": vm((q - EARLY * per, 2 * CAP, 128), BF16),
        "pre": vm((NX, EARLY * per, 2 * CAP, 128), BF16),
        "gath": vm((NX, q, 2 * CAP, 128), BF16),
        "wg": vm((2, model, hid), BF16),
        "wu": vm((2, model, hid), BF16),
        "wd": vm((2, hid, model), BF16),
        "abuf": vm((crow, model), BF16),
        "hbuf": vm((crow, 2 * hid), BF16),
        "ybuf": vm((chunks, NX, crow, 256), F32),
        "rs_s": vm((chunks, 3, 2, hrow, 256), BF16),
        "rs_r": vm((chunks, 3, 2, hrow, 256), BF16),
        "back": vm((q, 2 * CAP, 128), BF16),
        "ret": vm((q, 2 * CAP, 128), BF16),
        "macc": vm((2, rows, 128), F32),
        "mix_r": vm((rows, 128), F32),
        "st_ss": sem((2,)),
        "st_rs": sem((2,)),
        "one_ss": sem((3,)),
        "one_rs": sem((3,)),
        "edge_ss": sem((2,)),
        "edge_rs": sem((2,)),
        "wl": sem((3,)),
        "w_ss": sem((3,)),
        "w_rs": sem((3,)),
        "p_ss": sem((1,)),
        "p_rs": sem((2,)),
        "a_ss": sem((2,)),
        "a_rs": sem((chunks,)),
        "g_ss": sem((1,)),
        "g_rs": sem((chunks - EARLY, 2)),
        "r_ss": sem((1,)),
        "r_rs": sem((chunks, 2)),
        "b_ss": sem((1,)),
        "b_rs": sem((chunks,)),
    }


def kernel(keys, *refs):
    inputs, (wg_hbm, wu_hbm, wd_hbm, out_ref) = refs[:7], refs[7:11]
    s = types.SimpleNamespace(**dict(zip(keys, refs[11:])))
    frames_ref, taps_ref, cgain_ref, fgain_ref = s.frames, s.taps, s.cgain, s.fgain
    lengths_ref, routes_ref, rw_ref = s.lens, s.routes, s.rw
    brought = [
        pltpu.make_async_copy(src, dst, s.in_sem.at[i])
        for i, (src, dst) in enumerate(
            zip(inputs, (lengths_ref, frames_ref, taps_ref, cgain_ref, fgain_ref, routes_ref, rw_ref))
        )
    ]
    for i in (1, 0, 2, 3, 4, 5, 6):
        brought[i].start()
    rows, width = frames_ref.shape
    taps = taps_ref.shape[0]
    half = (taps - 1) // 2
    n_tm = NZ * NY
    n_t = 2 * NX
    model = width * n_t
    chunks = NZ
    per = NY // 2
    crow = per * CAP
    hrow = crow // 2
    groups = rows // 128

    tm = lax.axis_index("tm")
    ten = lax.axis_index("tensor")
    mz, my = div(tm, NY), rem(tm, NY)
    mx, mc = div(ten, 2), rem(ten, 2)
    oc = 1 - mc
    par = rem(my + mc, 2)
    own_k = ORDER.index(0)
    late = chunks - EARLY
    xr, xl, xo = rem(mx + 1, NX), rem(mx + NX - 1, NX), rem(mx + 2, NX)
    peer_t = mx * 2 + rem(my, 2)
    partner = (tm, mx * 2 + oc)
    right, left = (tm, xr * 2 + mc), (tm, xl * 2 + mc)
    sides = (rem(tm + n_tm - 1, n_tm), rem(tm + 1, n_tm))

    def turn_of(k):
        turn = jnp.int32(ORDER[0])
        for m in range(1, NZ):
            turn = turn + (ORDER[m] - ORDER[m - 1]) * div(k + NZ - m, NZ)
        return turn

    def dest(turn, i):
        return (rem(mz + 2 * i + turn, NZ) * NY + rem(my + 2 * i + par, NY), peer_t)

    def source(turn, i):
        return (rem(mz + 2 * NZ - 2 * i - turn, NZ) * NY + rem(my + 2 * NY - 2 * i - par, NY), peer_t)

    def per_block(k, remotely, locally=None):
        turn = turn_of(k)
        for i in range(per):
            if i > 0:
                remotely(k, turn, i)
                continue

            @pl.when((k != own_k) | (par > 0))
            def _():
                remotely(k, turn, 0)

            if locally is not None:

                @pl.when((k == own_k) & (par == 0))
                def _():
                    locally(k)

    def tensor_peer(d):
        return (tm, rem(ten + d, n_t))

    bar = pltpu.get_barrier_semaphore()

    def greet(dev):
        pl.semaphore_signal(bar, inc=1, device_id=dev, device_id_type=MESH)

    for d in range(1, n_t):
        greet(tensor_peer(d))
    for side in sides:
        for d in range(n_t):
            greet((side, rem(ten + d, n_t)))

    @pl.loop(0, chunks)
    def _(k):
        per_block(k, lambda k, turn, i: greet(dest(turn, i)))

    hbm = (wg_hbm, wu_hbm, wd_hbm)
    wbuf = (s.wg, s.wu, s.wd)
    local_w = [pltpu.make_async_copy(hbm[i], wbuf[i].at[0], s.wl.at[i]) for i in range(3)]
    for copy in local_w:
        copy.start()
    brought[1].wait()
    row_sums(frames_ref, s.stat_s.at[0], groups)
    for i in (0, 2, 3, 4, 5, 6):
        brought[i].wait()
    s.gain_s[...] = jnp.broadcast_to(fgain_ref[...], (8, 128))
    pl.semaphore_wait(bar, n_t - 1 + 2 * n_t + chunks * per - 1 + par)

    def stat_copies(phase):
        return [
            remote(s.stat_s.at[phase], s.stat_r.at[phase, d - 1], s.st_ss.at[phase], s.st_rs.at[phase], tensor_peer(d))
            for d in range(1, n_t)
        ]

    def factors(tiles):
        total = tiles[0]
        for tile in tiles[1:]:
            total = total + tile
        mean = total[0:groups] / model
        square = total[groups : 2 * groups] / model
        return mean, lax.rsqrt(square - mean * mean + EPS)

    def norm_factors(phase):
        return factors([s.stat_s[phase]] + [s.stat_r[phase, d] for d in range(n_t - 1)])

    first_stats = stat_copies(0)
    halos = [
        remote(s.frames.at[pl.ds(i * (rows - 16), 16)], s.halo_r.at[1 - i], s.edge_ss.at[0], s.edge_rs.at[0], (sides[i], ten))
        for i in range(2)
    ]
    edges = [
        remote(s.stat_s.at[0], s.edge_r.at[1 - i, d], s.edge_ss.at[1], s.edge_rs.at[1], (sides[i], rem(ten + d, n_t)))
        for i in range(2)
        for d in range(n_t)
    ]
    for copy in first_stats + halos + edges:
        copy.start()
    gain_copy = remote(s.gain_s, s.gain_r, s.one_ss.at[0], s.one_rs.at[0], partner)
    gain_copy.start()
    remote_w = [remote(hbm[i], wbuf[i].at[1], s.w_ss.at[i], s.w_rs.at[i], partner) for i in range(3)]
    for copy in remote_w:
        copy.start()

    s.tapf[0:taps, :] = taps_ref[...].astype(F32)
    starts = [jnp.int32(0)]
    for i in range(lengths_ref.shape[0]):
        starts.append(starts[-1] + lengths_ref[i])

    @pl.loop(0, groups)
    def _(g):
        r0 = pl.multiple_of(g * 128, 128)
        pos = tm * rows + r0 + lax.broadcasted_iota(I32, (128, 128), 0)
        begin = jnp.zeros((128, 128), I32)
        end = jnp.full((128, 128), n_tm * rows, I32)
        for i in range(1, len(starts) - 1):
            begin = jnp.where(pos >= starts[i], starts[i], begin)
        for i in range(len(starts) - 2, 0, -1):
            end = jnp.where(pos < starts[i], starts[i], end)
        s.behind[pl.ds(r0, 128), :] = pos - begin
        s.ahead[pl.ds(r0, 128), :] = end - 1 - pos

    n_exp = n_tm
    names_k = [routes_ref[0:1, :], routes_ref[1:2, :]]
    experts = lax.broadcasted_iota(I32, (n_exp, rows), 0)
    hot = [experts == name for name in names_k]
    both = jnp.where(hot[0] | hot[1], 1.0, 0.0).astype(BF16)
    upper = jnp.where(
        lax.broadcasted_iota(I32, (rows, rows), 0) < lax.broadcasted_iota(I32, (rows, rows), 1), 1.0, 0.0
    ).astype(BF16)
    earlier = jnp.dot(both, upper, preferred_element_type=F32)
    target = []
    for k in range(2):
        slot = jnp.sum(jnp.where(hot[k], earlier, 0.0), axis=0, keepdims=True).astype(I32)
        ez, ey = names_k[k] >> 3, names_k[k] & 7
        dz = (ez - mz + NZ) & (NZ - 1)
        dy = (ey - my + NY) & (NY - 1)
        turn = jnp.zeros(dz.shape, I32)
        for m in range(1, NZ):
            turn = jnp.where(((dz - 2 * (dy >> 1)) & (NZ - 1)) == ORDER[m], m, turn)
        q = turn * per + (dy >> 1)
        target.append(jnp.where((dy & 1) == par, q * CAP + slot, -1))
    place = lax.broadcasted_iota(I32, (crow, rows), 0)

    @pl.loop(0, chunks)
    def _(k):
        here = place + k * crow
        s.pmat[k] = jnp.where((here == target[0]) | (here == target[1]), 1.0, 0.0).astype(BF16)

    wait_all(s.stat_r.at[0], s.st_rs.at[0])

    mean, scale = norm_factors(0)
    for g in range(groups):
        x = frames_ref[128 * g : 128 * (g + 1), :].astype(F32)
        n = ((x - spread(mean[g : g + 1])) * spread(scale[g : g + 1]) * cgain_ref[...]).astype(BF16)
        s.nbuf[16 + 128 * g : 16 + 128 * (g + 1), :] = n.astype(F32)
    block = 64

    def conv(r0):
        acc = jnp.zeros((block, 128), F32)
        back_n = s.behind[pl.ds(r0, block), :]
        ahead_n = s.ahead[pl.ds(r0, block), :]
        for j in range(taps):
            d = j - half
            term = s.nbuf[pl.ds(r0 + 16 + d, block), :] * s.tapf[j : j + 1, :]
            if d < 0:
                term = jnp.where(back_n >= -d, term, 0.0)
            if d > 0:
                term = jnp.where(ahead_n >= d, term, 0.0)
            acc = acc + term
        x = frames_ref[pl.ds(r0, block), :].astype(F32)
        s.resid[pl.ds(r0, block), :] = x + acc / (1.0 + jnp.exp(-acc))

    for r0 in range(block, rows - block, block):
        conv(r0)
    wait_all(s.halo_r, s.edge_rs.at[0])
    wait_all(s.edge_r, s.edge_rs.at[1])
    for i, g in enumerate((groups - 1, 0)):
        mean, scale = factors([s.edge_r[i, d] for d in range(n_t)])
        span = slice(112, 128) if i == 0 else slice(0, 16)
        x = s.halo_r[i].astype(F32)
        n = ((x - spread(mean[g : g + 1])[span]) * spread(scale[g : g + 1])[span] * cgain_ref[...]).astype(BF16)
        s.nbuf[i * (rows + 16) : i * (rows + 16) + 16, :] = n.astype(F32)
    conv(0)
    conv(rows - block)

    resid_copy = remote(s.resid, s.resid_p, s.one_ss.at[1], s.one_rs.at[1], partner)
    resid_copy.start()
    row_sums(s.resid, s.stat_s.at[1], groups)
    second_stats = stat_copies(1)
    for copy in second_stats:
        copy.start()

    for k in range(2):
        for g in range(groups):
            lanes = slice(128 * g, 128 * (g + 1))
            s.dcol[k, lanes, :] = spread(target[k][:, lanes].astype(F32)).astype(I32)
            s.wcol[k, lanes, :] = spread(rw_ref[k : k + 1, lanes])

    gain_copy.wait_recv()
    resid_copy.wait_recv()
    wait_all(s.stat_r.at[1], s.st_rs.at[1])
    mean, scale = norm_factors(1)
    for g in range(groups):
        m, r = spread(mean[g : g + 1]), spread(scale[g : g + 1])
        lanes = pl.ds(128 * g, 128)
        s.ein[mc, lanes, :] = ((s.resid[lanes, :] - m) * r * fgain_ref[...]).astype(BF16)
        s.ein[oc, lanes, :] = ((s.resid_p[lanes, :] - m) * r * s.gain_r[0:1, :]).astype(BF16)

    def send(k, turn, i):
        q = k * per + i
        remote(s.table.at[q], s.gath.at[mx, q], s.a_ss.at[0], s.a_rs.at[k], dest(turn, i)).start()

    def keep(k):
        pltpu.make_async_copy(s.table.at[k * per], s.gath.at[mx, k * per], s.a_rs.at[k]).start()

    def pack(value):
        v = jnp.concatenate([value[:, 0:128].reshape(per, CAP, 128), value[:, 128:256].reshape(per, CAP, 128)], axis=1)
        return v.astype(BF16)

    def unpack(value):
        v = value.astype(F32)
        return v[:, :CAP, :].reshape(crow, 128).astype(BF16), v[:, CAP:, :].reshape(crow, 128).astype(BF16)

    def picked(k):
        both_cols = jnp.concatenate([s.ein[0], s.ein[1]], axis=1)
        return pack(jnp.dot(s.pmat[k], both_cols, preferred_element_type=F32))

    def early_copy(x, span, i, dev):
        return remote(s.pre.at[x, span], s.pre.at[x, span], s.p_ss.at[0], s.p_rs.at[i], dev)

    def send_early(k, turn, i):
        q = k * per + i
        remote(s.pre.at[:, q - late * per], s.gath.at[:, q], s.a_ss.at[1], s.a_rs.at[k], dest(turn, i)).start()

    @pl.loop(late, chunks)
    def _(k):
        s.pre[mx, pl.ds((k - late) * per, per)] = picked(k)

    n_early = EARLY * per
    early_copy(mx, pl.ds(0, n_early), 0, right).start()
    early_copy(mx, pl.ds(0, n_early), 0, left).start()

    def dispatch(k):
        s.table[pl.ds(k * per, per)] = picked(k)
        per_block(k, send, keep)

    @pl.loop(0, late)
    def _(k):
        dispatch(k)

    @pl.loop(0, chunks)
    def _(k):
        here = k * crow + lax.broadcasted_iota(I32, (128, crow), 1)
        for g in range(groups):
            lanes = slice(128 * g, 128 * (g + 1))
            w = jnp.where(here == s.dcol[0, lanes, 0:1], s.wcol[0, lanes, 0:1], 0.0)
            w = w + jnp.where(here == s.dcol[1, lanes, 0:1], s.wcol[1, lanes, 0:1], 0.0)
            high = w.astype(BF16)
            s.wmat[k, 0, lanes, :] = high
            s.wmat[k, 1, lanes, :] = (w - high.astype(F32)).astype(BF16)

    s.macc[...] = jnp.zeros(s.macc.shape, F32)

    def gather_copies(k):
        whole, first, second = pl.ds(k * per, per), pl.ds(k * per, per // 2), pl.ds(k * per + per // 2, per // 2)

        def along(x, span, i, dev):
            return remote(s.gath.at[x, span], s.gath.at[x, span], s.g_ss.at[0], s.g_rs.at[k, i // 2], dev)

        return (
            along(mx, whole, 0, right),
            along(mx, whole, 1, left),
            along(xl, first, 2, right),
            along(xr, second, 3, left),
        )

    def sum_copy(k, way, i):
        return remote(s.rs_s.at[k, i, way], s.rs_r.at[k, i, way], s.r_ss.at[0], s.r_rs.at[k, min(i, 1)], (right, left)[way])

    def send_back(k, turn, i):
        q = k * per + i
        remote(s.back.at[q], s.ret.at[q], s.b_ss.at[0], s.b_rs.at[k], source(turn, i)).start()

    def keep_back(k):
        pltpu.make_async_copy(s.back.at[k * per], s.ret.at[k * per], s.b_rs.at[k]).start()

    for copy in local_w:
        copy.wait()
    for copy in remote_w:
        copy.wait_recv()

    def leave_early():
        wait_all(s.pre.at[0], s.p_rs.at[1])

        @pl.loop(late, chunks)
        def _(k):
            per_block(k, send_early)

    def arrive(k):
        wait_all(s.gath.at[mx, pl.ds(k * per, per)], s.a_rs.at[k])
        to_right, to_left, _, _ = gather_copies(k)
        to_right.start()
        to_left.start()

    def forward(k):
        _, _, on_right, on_left = gather_copies(k)
        wait_all(s.gath.at[pl.ds(0, 2), pl.ds(k * per, per)], s.g_rs.at[k, 0])
        on_right.start()
        on_left.start()

    def experts_of(k):
        @pl.when(k < late)
        def _():
            wait_all(s.gath.at[0, pl.ds(k * per, per)], s.g_rs.at[k, 1])

        @pl.when(k >= late)
        def _():
            wait_all(s.gath.at[:, pl.ds(k * per, per)], s.a_rs.at[k])

        for x in range(NX):
            low, high = unpack(s.gath[x, pl.ds(k * per, per)])
            s.abuf[:, 256 * x : 256 * x + 128] = low
            s.abuf[:, 256 * x + 128 : 256 * x + 256] = high
        hid = s.wg.shape[2]
        for c in range(2):
            for n in range(0, hid, 256):
                gate = jnp.dot(s.abuf[...], s.wg[c, :, n : n + 256], preferred_element_type=F32)
                up = jnp.dot(s.abuf[...], s.wu[c, :, n : n + 256], preferred_element_type=F32)
                s.hbuf[:, hid * c + n : hid * c + n + 256] = (gate / (1.0 + jnp.exp(-gate)) * up).astype(BF16)
        for n in range(NX):
            cols = slice(256 * n, 256 * (n + 1))
            y = jnp.dot(s.hbuf[:, :hid], s.wd[0, :, cols], preferred_element_type=F32)
            s.ybuf[k, n] = y + jnp.dot(s.hbuf[:, hid:], s.wd[1, :, cols], preferred_element_type=F32)
        s.rs_s[k, 0, 0] = s.ybuf[k, xo, 0:hrow, :].astype(BF16)
        sum_copy(k, 0, 0).start()
        s.rs_s[k, 0, 1] = s.ybuf[k, xo, hrow:crow, :].astype(BF16)
        sum_copy(k, 1, 0).start()
        s.rs_s[k, 1, 0] = s.ybuf[k, xr, hrow:crow, :].astype(BF16)
        sum_copy(k, 0, 1).start()
        s.rs_s[k, 1, 1] = s.ybuf[k, xl, 0:hrow, :].astype(BF16)
        sum_copy(k, 1, 1).start()

    def pass_on(k):
        wait_all(s.rs_r.at[k, 0], s.r_rs.at[k, 0])
        s.rs_s[k, 2, 0] = (s.ybuf[k, xr, 0:hrow, :] + s.rs_r[k, 0, 0].astype(F32)).astype(BF16)
        sum_copy(k, 0, 2).start()
        s.rs_s[k, 2, 1] = (s.ybuf[k, xl, hrow:crow, :] + s.rs_r[k, 0, 1].astype(F32)).astype(BF16)
        sum_copy(k, 1, 2).start()

    def finish(k):
        wait_all(s.rs_r.at[k, pl.ds(1, 2)], s.r_rs.at[k, 1])
        top = s.ybuf[k, mx, 0:hrow, :] + s.rs_r[k, 2, 0].astype(F32) + s.rs_r[k, 1, 1].astype(F32)
        low = s.ybuf[k, mx, hrow:crow, :] + s.rs_r[k, 2, 1].astype(F32) + s.rs_r[k, 1, 0].astype(F32)
        s.back[pl.ds(k * per, per)] = pack(jnp.concatenate([top, low], axis=0))
        per_block(k, send_back, keep_back)

    def combine(k):
        wait_all(s.ret.at[pl.ds(k * per, per)], s.b_rs.at[k])
        low, high = unpack(s.ret[pl.ds(k * per, per)])
        both_cols = jnp.concatenate([low, high], axis=1)
        mixed = jnp.dot(s.wmat[k, 0], both_cols, preferred_element_type=F32)
        mixed = mixed + jnp.dot(s.wmat[k, 1], both_cols, preferred_element_type=F32)
        s.macc[0] += mixed[:, 0:128]
        s.macc[1] += mixed[:, 128:256]

    def at(step, lag, stage, count=chunks):
        @pl.when((step >= lag) & (step < lag + count))
        def _():
            stage(step - lag)

    wait_all(s.pre.at[pl.ds(0, 2)], s.p_rs.at[0])
    early_copy(xl, pl.ds(0, n_early // 2), 1, right).start()
    early_copy(xr, pl.ds(n_early // 2, n_early // 2), 1, left).start()

    @pl.loop(0, chunks + LAGS[4])
    def _(step):
        pl.when(step == SEND_EARLY)(leave_early)
        at(step, 0, arrive, late)
        at(step, LAGS[0], forward, late)
        at(step, LAGS[2], pass_on)
        at(step, LAGS[3], finish)
        at(step, LAGS[1], experts_of)
        at(step, LAGS[4], combine)

    mix_copy = remote(s.macc.at[oc], s.mix_r, s.one_ss.at[2], s.one_rs.at[2], partner)
    mix_copy.start()
    own = s.resid[...] + s.macc[mc]
    mix_copy.wait_recv()
    out_ref[...] = (own + s.mix_r[...]).astype(BF16)

    for copy in [gain_copy, resid_copy, mix_copy] + remote_w:
        copy.wait_send()
    for phase in range(2):
        wait_all(s.stat_r.at[phase], s.st_ss.at[phase])
    wait_all(s.halo_r, s.edge_ss.at[0])
    wait_all(s.edge_r, s.edge_ss.at[1])
    wait_all(s.gath.at[pl.ds(0, 3), pl.ds(0, late * per)], s.g_ss.at[0])
    wait_all(s.pre.at[pl.ds(0, 3)], s.p_ss.at[0])
    wait_all(s.pre, s.a_ss.at[1])
    wait_all(s.rs_s, s.r_ss.at[0])
    wait_all(s.table.at[pl.ds(0, late * per - 1)], s.a_ss.at[0])
    wait_all(s.back.at[pl.ds(0, chunks * per - 1)], s.b_ss.at[0])

    @pl.when(par > 0)
    def _():
        wait_all(s.table.at[0], s.a_ss.at[0])
        wait_all(s.back.at[0], s.b_ss.at[0])


def shards(frames, conv_kernel, conv_gain, ffn_gain, lengths, routes, route_weights, w_gate, w_up, w_down):
    rows, width = frames.shape
    _, depth, hid = w_gate.shape
    scratch = names(rows, width, hid, depth, conv_kernel.shape[0], lengths.shape[0])
    vmem = pl.BlockSpec(memory_space=pltpu.VMEM)
    return pl.pallas_call(
        functools.partial(kernel, tuple(scratch)),
        out_shape=jax.ShapeDtypeStruct((rows, width), BF16),
        in_specs=[pl.BlockSpec(memory_space=pl.ANY)] * 10,
        out_specs=vmem,
        scratch_shapes=list(scratch.values()),
        compiler_params=pltpu.CompilerParams(collective_id=0, has_side_effects=True, vmem_limit_bytes=56 * 1024 * 1024),
    )(
        lengths,
        frames,
        conv_kernel,
        conv_gain.reshape(1, width),
        ffn_gain.reshape(1, width),
        routes.T,
        route_weights.T,
        w_gate.reshape(depth, hid),
        w_up.reshape(depth, hid),
        w_down.reshape(hid, depth),
    )


def solution(mesh):
    in_specs = (
        P("tm", "tensor"),
        P(None, "tensor"),
        P("tensor"),
        P("tensor"),
        P(),
        P("tm", None),
        P("tm", None),
        P("tm", None, "tensor"),
        P("tm", None, "tensor"),
        P("tm", "tensor", None),
    )
    return jax.shard_map(shards, mesh=mesh, in_specs=in_specs, out_specs=P("tm", "tensor"), check_vma=False)
```

```python
import functools
import types

import jax
import jax.numpy as jnp
from jax import lax
from jax.experimental import pallas as pl
from jax.experimental.pallas import tpu as pltpu
from jax.sharding import PartitionSpec as P

MESH = pl.DeviceIdType.MESH
EPS = 1e-05
CAP = 24
NX = 4
NZ = 8
NY = 8
ORDER = (0, 7, 1, 3, 5, 2, 6, 4)
EARLY = 2
SEND_EARLY = 2
LAGS = (3, 6, 9, 12, 21)
F32 = jnp.float32
BF16 = jnp.bfloat16
I32 = jnp.int32


def div(a, b):
    return lax.div(a, jnp.int32(b))


def rem(a, b):
    return lax.rem(a, jnp.int32(b))


def remote(src, dst, ss, rs, dev):
    return pltpu.make_async_remote_copy(
        src_ref=src, dst_ref=dst, send_sem=ss, recv_sem=rs, device_id=dev, device_id_type=MESH
    )


def wait_all(ref, sem):
    pltpu.make_async_copy(ref, ref, sem).wait()


def spread(row):
    return jnp.broadcast_to(row, (128, 128)).T


def row_sums(value_ref, dst_ref, groups):
    for g in range(groups):
        v = value_ref[128 * g : 128 * (g + 1), :].astype(F32).T
        dst_ref[g : g + 1, :] = jnp.sum(v, axis=0, keepdims=True)
        dst_ref[groups + g : groups + g + 1, :] = jnp.sum(v * v, axis=0, keepdims=True)


def names(rows, width, hid, depth, taps, lens):
    groups = rows // 128
    chunks, per = NZ, NY // 2
    q = chunks * per
    crow = per * CAP
    hrow = crow // 2
    model = width * 2 * NX
    vm = pltpu.VMEM
    sem = pltpu.SemaphoreType.DMA
    return {
        "lens": pltpu.SMEM((lens,), I32),
        "frames": vm((rows, width), BF16),
        "taps": vm((taps, width), BF16),
        "cgain": vm((1, width), F32),
        "fgain": vm((1, width), F32),
        "routes": vm((2, rows), I32),
        "rw": vm((2, rows), F32),
        "in_sem": sem((7,)),
        "stat_s": vm((2, 2 * groups, 128), F32),
        "stat_r": vm((2, 2 * NX - 1, 2 * groups, 128), F32),
        "gain_s": vm((8, 128), F32),
        "gain_r": vm((8, 128), F32),
        "nbuf": vm((rows + 32, 128), F32),
        "edge_r": vm((2, 2 * NX, 2 * groups, 128), F32),
        "halo_r": vm((2, 16, 128), BF16),
        "behind": vm((rows, 128), I32),
        "ahead": vm((rows, 128), I32),
        "tapf": vm((32, 128), F32),
        "resid": vm((rows, 128), F32),
        "resid_p": vm((rows, 128), F32),
        "ein": vm((2, rows, 128), BF16),
        "pmat": vm((chunks, crow, rows), BF16),
        "dcol": vm((2, rows, 128), I32),
        "wcol": vm((2, rows, 128), F32),
        "wmat": vm((chunks, 2, rows, crow), BF16),
        "table": vm((q - EARLY * per, 2 * CAP, 128), BF16),
        "pre": vm((NX, EARLY * per, 2 * CAP, 128), BF16),
        "gath": vm((NX, q, 2 * CAP, 128), BF16),
        "wg": vm((2, model, hid), BF16),
        "wu": vm((2, model, hid), BF16),
        "wd": vm((2, hid, model), BF16),
        "abuf": vm((crow, model), BF16),
        "hbuf": vm((crow, 2 * hid), BF16),
        "ybuf": vm((chunks, NX, crow, 256), F32),
        "rs_s": vm((chunks, 3, 2, hrow, 256), BF16),
        "rs_r": vm((chunks, 3, 2, hrow, 256), BF16),
        "back": vm((q, 2 * CAP, 128), BF16),
        "ret": vm((q, 2 * CAP, 128), BF16),
        "macc": vm((2, rows, 128), F32),
        "mix_s": vm((rows, 128), BF16),
        "mix_r": vm((rows, 128), BF16),
        "st_ss": sem((2,)),
        "st_rs": sem((2,)),
        "one_ss": sem((3,)),
        "one_rs": sem((3,)),
        "edge_ss": sem((2,)),
        "edge_rs": sem((2,)),
        "w_sem": sem((3,)),
        "p_ss": sem((1,)),
        "p_rs": sem((2,)),
        "a_ss": sem((2,)),
        "a_rs": sem((chunks,)),
        "g_ss": sem((1,)),
        "g_rs": sem((chunks - EARLY, 2)),
        "r_ss": sem((1,)),
        "r_rs": sem((chunks, 2)),
        "b_ss": sem((1,)),
        "b_rs": sem((chunks,)),
    }


def kernel(keys, *refs):
    inputs, (wg_hbm, wu_hbm, wd_hbm, out_ref) = refs[:7], refs[7:11]
    s = types.SimpleNamespace(**dict(zip(keys, refs[11:])))
    frames_ref, taps_ref, cgain_ref, fgain_ref = s.frames, s.taps, s.cgain, s.fgain
    lengths_ref, routes_ref, rw_ref = s.lens, s.routes, s.rw
    brought = [
        pltpu.make_async_copy(src, dst, s.in_sem.at[i])
        for i, (src, dst) in enumerate(
            zip(inputs, (lengths_ref, frames_ref, taps_ref, cgain_ref, fgain_ref, routes_ref, rw_ref))
        )
    ]
    for i in (1, 0, 2, 3, 4, 5, 6):
        brought[i].start()
    rows, width = frames_ref.shape
    taps = taps_ref.shape[0]
    half = (taps - 1) // 2
    n_tm = NZ * NY
    n_t = 2 * NX
    model = width * n_t
    chunks = NZ
    per = NY // 2
    crow = per * CAP
    hrow = crow // 2
    groups = rows // 128

    tm = lax.axis_index("tm")
    ten = lax.axis_index("tensor")
    mz, my = div(tm, NY), rem(tm, NY)
    mx, mc = div(ten, 2), rem(ten, 2)
    oc = 1 - mc
    par = rem(my + mc, 2)
    own_k = ORDER.index(0)
    late = chunks - EARLY
    xr, xl, xo = rem(mx + 1, NX), rem(mx + NX - 1, NX), rem(mx + 2, NX)
    peer_t = mx * 2 + rem(my, 2)
    partner = (tm, mx * 2 + oc)
    right, left = (tm, xr * 2 + mc), (tm, xl * 2 + mc)
    sides = (rem(tm + n_tm - 1, n_tm), rem(tm + 1, n_tm))

    def turn_of(k):
        turn = jnp.int32(ORDER[0])
        for m in range(1, NZ):
            turn = turn + (ORDER[m] - ORDER[m - 1]) * div(k + NZ - m, NZ)
        return turn

    def dest(turn, i):
        return (rem(mz + 2 * i + turn, NZ) * NY + rem(my + 2 * i + par, NY), peer_t)

    def source(turn, i):
        return (rem(mz + 2 * NZ - 2 * i - turn, NZ) * NY + rem(my + 2 * NY - 2 * i - par, NY), peer_t)

    def per_block(k, remotely, locally=None):
        turn = turn_of(k)
        for i in range(per):
            if i > 0:
                remotely(k, turn, i)
                continue

            @pl.when((k != own_k) | (par > 0))
            def _():
                remotely(k, turn, 0)

            if locally is not None:

                @pl.when((k == own_k) & (par == 0))
                def _():
                    locally(k)

    def tensor_peer(d):
        return (tm, rem(ten + d, n_t))

    bar = pltpu.get_barrier_semaphore()

    def greet(dev):
        pl.semaphore_signal(bar, inc=1, device_id=dev, device_id_type=MESH)

    for d in range(1, n_t):
        greet(tensor_peer(d))
    for side in sides:
        for d in range(n_t):
            greet((side, rem(ten + d, n_t)))

    @pl.loop(0, chunks)
    def _(k):
        per_block(k, lambda k, turn, i: greet(dest(turn, i)))

    hbm = (wg_hbm, wu_hbm, wd_hbm)
    wbuf = (s.wg, s.wu, s.wd)
    local_w = [pltpu.make_async_copy(hbm[i], wbuf[i].at[0], s.w_sem.at[0]) for i in range(3)]
    for copy in local_w:
        copy.start()
    brought[1].wait()
    row_sums(frames_ref, s.stat_s.at[0], groups)
    for i in (0, 2, 3, 4, 5, 6):
        brought[i].wait()
    s.gain_s[...] = jnp.broadcast_to(fgain_ref[...], (8, 128))
    pl.semaphore_wait(bar, n_t - 1 + 2 * n_t + chunks * per - 1 + par)

    def stat_copies(phase):
        return [
            remote(s.stat_s.at[phase], s.stat_r.at[phase, d - 1], s.st_ss.at[phase], s.st_rs.at[phase], tensor_peer(d))
            for d in range(1, n_t)
        ]

    def factors(tiles):
        total = tiles[0]
        for tile in tiles[1:]:
            total = total + tile
        mean = total[0:groups] / model
        square = total[groups : 2 * groups] / model
        return mean, lax.rsqrt(square - mean * mean + EPS)

    def norm_factors(phase):
        return factors([s.stat_s[phase]] + [s.stat_r[phase, d] for d in range(n_t - 1)])

    first_stats = stat_copies(0)
    halos = [
        remote(s.frames.at[pl.ds(i * (rows - 16), 16)], s.halo_r.at[1 - i], s.edge_ss.at[0], s.edge_rs.at[0], (sides[i], ten))
        for i in range(2)
    ]
    edges = [
        remote(s.stat_s.at[0], s.edge_r.at[1 - i, d], s.edge_ss.at[1], s.edge_rs.at[1], (sides[i], rem(ten + d, n_t)))
        for i in range(2)
        for d in range(n_t)
    ]
    for copy in first_stats + halos + edges:
        copy.start()
    gain_copy = remote(s.gain_s, s.gain_r, s.one_ss.at[0], s.one_rs.at[0], partner)
    gain_copy.start()
    remote_w = [remote(hbm[i], wbuf[i].at[1], s.w_sem.at[1], s.w_sem.at[2], partner) for i in range(3)]
    for copy in remote_w:
        copy.start()

    s.tapf[0:taps, :] = taps_ref[...].astype(F32)
    starts = [jnp.int32(0)]
    for i in range(lengths_ref.shape[0]):
        starts.append(starts[-1] + lengths_ref[i])

    @pl.loop(0, groups)
    def _(g):
        r0 = pl.multiple_of(g * 128, 128)
        pos = tm * rows + r0 + lax.broadcasted_iota(I32, (128, 128), 0)
        begin = jnp.zeros((128, 128), I32)
        end = jnp.full((128, 128), n_tm * rows, I32)
        for i in range(1, len(starts) - 1):
            begin = jnp.where(pos >= starts[i], starts[i], begin)
        for i in range(len(starts) - 2, 0, -1):
            end = jnp.where(pos < starts[i], starts[i], end)
        s.behind[pl.ds(r0, 128), :] = pos - begin
        s.ahead[pl.ds(r0, 128), :] = end - 1 - pos

    n_exp = n_tm
    names_k = [routes_ref[0:1, :], routes_ref[1:2, :]]
    experts = lax.broadcasted_iota(I32, (n_exp, rows), 0)
    hot = [experts == name for name in names_k]
    both = jnp.where(hot[0] | hot[1], 1.0, 0.0).astype(BF16)
    upper = jnp.where(
        lax.broadcasted_iota(I32, (rows, rows), 0) < lax.broadcasted_iota(I32, (rows, rows), 1), 1.0, 0.0
    ).astype(BF16)
    earlier = jnp.dot(both, upper, preferred_element_type=F32)
    target = []
    for k in range(2):
        slot = jnp.sum(jnp.where(hot[k], earlier, 0.0), axis=0, keepdims=True).astype(I32)
        ez, ey = names_k[k] >> 3, names_k[k] & 7
        dz = (ez - mz + NZ) & (NZ - 1)
        dy = (ey - my + NY) & (NY - 1)
        turn = jnp.zeros(dz.shape, I32)
        for m in range(1, NZ):
            turn = jnp.where(((dz - 2 * (dy >> 1)) & (NZ - 1)) == ORDER[m], m, turn)
        q = turn * per + (dy >> 1)
        target.append(jnp.where((dy & 1) == par, q * CAP + slot, -1))
    place = lax.broadcasted_iota(I32, (crow, rows), 0)

    @pl.loop(0, chunks)
    def _(k):
        here = place + k * crow
        s.pmat[k] = jnp.where((here == target[0]) | (here == target[1]), 1.0, 0.0).astype(BF16)

    wait_all(s.stat_r.at[0], s.st_rs.at[0])

    mean, scale = norm_factors(0)
    for g in range(groups):
        x = frames_ref[128 * g : 128 * (g + 1), :].astype(F32)
        n = ((x - spread(mean[g : g + 1])) * spread(scale[g : g + 1]) * cgain_ref[...]).astype(BF16)
        s.nbuf[16 + 128 * g : 16 + 128 * (g + 1), :] = n.astype(F32)
    block = 64

    def conv(r0):
        acc = jnp.zeros((block, 128), F32)
        back_n = s.behind[pl.ds(r0, block), :]
        ahead_n = s.ahead[pl.ds(r0, block), :]
        for j in range(taps):
            d = j - half
            term = s.nbuf[pl.ds(r0 + 16 + d, block), :] * s.tapf[j : j + 1, :]
            if d < 0:
                term = jnp.where(back_n >= -d, term, 0.0)
            if d > 0:
                term = jnp.where(ahead_n >= d, term, 0.0)
            acc = acc + term
        x = frames_ref[pl.ds(r0, block), :].astype(F32)
        s.resid[pl.ds(r0, block), :] = x + acc / (1.0 + jnp.exp(-acc))

    for r0 in range(block, rows - block, block):
        conv(r0)
    wait_all(s.halo_r, s.edge_rs.at[0])
    wait_all(s.edge_r, s.edge_rs.at[1])
    for i, g in enumerate((groups - 1, 0)):
        mean, scale = factors([s.edge_r[i, d] for d in range(n_t)])
        span = slice(112, 128) if i == 0 else slice(0, 16)
        x = s.halo_r[i].astype(F32)
        n = ((x - spread(mean[g : g + 1])[span]) * spread(scale[g : g + 1])[span] * cgain_ref[...]).astype(BF16)
        s.nbuf[i * (rows + 16) : i * (rows + 16) + 16, :] = n.astype(F32)
    conv(0)
    conv(rows - block)

    resid_copy = remote(s.resid, s.resid_p, s.one_ss.at[1], s.one_rs.at[1], partner)
    resid_copy.start()
    row_sums(s.resid, s.stat_s.at[1], groups)
    second_stats = stat_copies(1)
    for copy in second_stats:
        copy.start()

    for k in range(2):
        for g in range(groups):
            lanes = slice(128 * g, 128 * (g + 1))
            s.dcol[k, lanes, :] = spread(target[k][:, lanes].astype(F32)).astype(I32)
            s.wcol[k, lanes, :] = spread(rw_ref[k : k + 1, lanes])

    gain_copy.wait_recv()
    resid_copy.wait_recv()
    wait_all(s.stat_r.at[1], s.st_rs.at[1])
    mean, scale = norm_factors(1)
    for g in range(groups):
        m, r = spread(mean[g : g + 1]), spread(scale[g : g + 1])
        lanes = pl.ds(128 * g, 128)
        s.ein[mc, lanes, :] = ((s.resid[lanes, :] - m) * r * fgain_ref[...]).astype(BF16)
        s.ein[oc, lanes, :] = ((s.resid_p[lanes, :] - m) * r * s.gain_r[0:1, :]).astype(BF16)

    def send(k, turn, i):
        q = k * per + i
        remote(s.table.at[q], s.gath.at[mx, q], s.a_ss.at[0], s.a_rs.at[k], dest(turn, i)).start()

    def keep(k):
        pltpu.make_async_copy(s.table.at[k * per], s.gath.at[mx, k * per], s.a_rs.at[k]).start()

    def pack(value):
        v = jnp.concatenate([value[:, 0:128].reshape(per, CAP, 128), value[:, 128:256].reshape(per, CAP, 128)], axis=1)
        return v.astype(BF16)

    def unpack(value):
        v = value.astype(F32)
        return v[:, :CAP, :].reshape(crow, 128).astype(BF16), v[:, CAP:, :].reshape(crow, 128).astype(BF16)

    def picked(k):
        both_cols = jnp.concatenate([s.ein[0], s.ein[1]], axis=1)
        return pack(jnp.dot(s.pmat[k], both_cols, preferred_element_type=F32))

    def early_copy(x, span, i, dev):
        return remote(s.pre.at[x, span], s.pre.at[x, span], s.p_ss.at[0], s.p_rs.at[i], dev)

    def send_early(k, turn, i):
        q = k * per + i
        remote(s.pre.at[:, q - late * per], s.gath.at[:, q], s.a_ss.at[1], s.a_rs.at[k], dest(turn, i)).start()

    @pl.loop(late, chunks)
    def _(k):
        s.pre[mx, pl.ds((k - late) * per, per)] = picked(k)

    n_early = EARLY * per
    early_copy(mx, pl.ds(0, n_early), 0, right).start()
    early_copy(mx, pl.ds(0, n_early), 0, left).start()

    def dispatch(k):
        s.table[pl.ds(k * per, per)] = picked(k)
        per_block(k, send, keep)

    @pl.loop(0, late)
    def _(k):
        dispatch(k)

    @pl.loop(0, chunks)
    def _(k):
        here = k * crow + lax.broadcasted_iota(I32, (128, crow), 1)
        for g in range(groups):
            lanes = slice(128 * g, 128 * (g + 1))
            w = jnp.where(here == s.dcol[0, lanes, 0:1], s.wcol[0, lanes, 0:1], 0.0)
            w = w + jnp.where(here == s.dcol[1, lanes, 0:1], s.wcol[1, lanes, 0:1], 0.0)
            high = w.astype(BF16)
            s.wmat[k, 0, lanes, :] = high
            s.wmat[k, 1, lanes, :] = (w - high.astype(F32)).astype(BF16)

    s.macc[...] = jnp.zeros(s.macc.shape, F32)

    def gather_copies(k):
        whole, first, second = pl.ds(k * per, per), pl.ds(k * per, per // 2), pl.ds(k * per + per // 2, per // 2)

        def along(x, span, i, dev):
            return remote(s.gath.at[x, span], s.gath.at[x, span], s.g_ss.at[0], s.g_rs.at[k, i // 2], dev)

        return (
            along(mx, whole, 0, right),
            along(mx, whole, 1, left),
            along(xl, first, 2, right),
            along(xr, second, 3, left),
        )

    def sum_copy(k, way, i):
        return remote(s.rs_s.at[k, i, way], s.rs_r.at[k, i, way], s.r_ss.at[0], s.r_rs.at[k, min(i, 1)], (right, left)[way])

    def send_back(k, turn, i):
        q = k * per + i
        remote(s.back.at[q], s.ret.at[q], s.b_ss.at[0], s.b_rs.at[k], source(turn, i)).start()

    def keep_back(k):
        pltpu.make_async_copy(s.back.at[k * per], s.ret.at[k * per], s.b_rs.at[k]).start()

    wait_all(s.ybuf, s.w_sem.at[0])
    wait_all(s.ybuf, s.w_sem.at[2])

    def leave_early():
        wait_all(s.pre.at[0], s.p_rs.at[1])

        @pl.loop(late, chunks)
        def _(k):
            per_block(k, send_early)

    def arrive(k):
        wait_all(s.gath.at[mx, pl.ds(k * per, per)], s.a_rs.at[k])
        to_right, to_left, _, _ = gather_copies(k)
        to_right.start()
        to_left.start()

    def forward(k):
        _, _, on_right, on_left = gather_copies(k)
        wait_all(s.gath.at[pl.ds(0, 2), pl.ds(k * per, per)], s.g_rs.at[k, 0])
        on_right.start()
        on_left.start()

    def experts_of(k):
        @pl.when(k < late)
        def _():
            wait_all(s.gath.at[0, pl.ds(k * per, per)], s.g_rs.at[k, 1])

        @pl.when(k >= late)
        def _():
            wait_all(s.gath.at[:, pl.ds(k * per, per)], s.a_rs.at[k])

        for x in range(NX):
            low, high = unpack(s.gath[x, pl.ds(k * per, per)])
            s.abuf[:, 256 * x : 256 * x + 128] = low
            s.abuf[:, 256 * x + 128 : 256 * x + 256] = high
        hid = s.wg.shape[2]
        for c in range(2):
            for n in range(0, hid, 256):
                gate = jnp.dot(s.abuf[...], s.wg[c, :, n : n + 256], preferred_element_type=F32)
                up = jnp.dot(s.abuf[...], s.wu[c, :, n : n + 256], preferred_element_type=F32)
                s.hbuf[:, hid * c + n : hid * c + n + 256] = (gate / (1.0 + jnp.exp(-gate)) * up).astype(BF16)
        for n in range(NX):
            cols = slice(256 * n, 256 * (n + 1))
            y = jnp.dot(s.hbuf[:, :hid], s.wd[0, :, cols], preferred_element_type=F32)
            s.ybuf[k, n] = y + jnp.dot(s.hbuf[:, hid:], s.wd[1, :, cols], preferred_element_type=F32)
        s.rs_s[k, 0, 0] = s.ybuf[k, xo, 0:hrow, :].astype(BF16)
        sum_copy(k, 0, 0).start()
        s.rs_s[k, 0, 1] = s.ybuf[k, xo, hrow:crow, :].astype(BF16)
        sum_copy(k, 1, 0).start()
        s.rs_s[k, 1, 0] = s.ybuf[k, xr, hrow:crow, :].astype(BF16)
        sum_copy(k, 0, 1).start()
        s.rs_s[k, 1, 1] = s.ybuf[k, xl, 0:hrow, :].astype(BF16)
        sum_copy(k, 1, 1).start()

    def pass_on(k):
        wait_all(s.rs_r.at[k, 0], s.r_rs.at[k, 0])
        s.rs_s[k, 2, 0] = (s.ybuf[k, xr, 0:hrow, :] + s.rs_r[k, 0, 0].astype(F32)).astype(BF16)
        sum_copy(k, 0, 2).start()
        s.rs_s[k, 2, 1] = (s.ybuf[k, xl, hrow:crow, :] + s.rs_r[k, 0, 1].astype(F32)).astype(BF16)
        sum_copy(k, 1, 2).start()

    def finish(k):
        wait_all(s.rs_r.at[k, pl.ds(1, 2)], s.r_rs.at[k, 1])
        top = s.ybuf[k, mx, 0:hrow, :] + s.rs_r[k, 2, 0].astype(F32) + s.rs_r[k, 1, 1].astype(F32)
        low = s.ybuf[k, mx, hrow:crow, :] + s.rs_r[k, 2, 1].astype(F32) + s.rs_r[k, 1, 0].astype(F32)
        s.back[pl.ds(k * per, per)] = pack(jnp.concatenate([top, low], axis=0))
        per_block(k, send_back, keep_back)

    def combine(k):
        wait_all(s.ret.at[pl.ds(k * per, per)], s.b_rs.at[k])
        low, high = unpack(s.ret[pl.ds(k * per, per)])
        both_cols = jnp.concatenate([low, high], axis=1)
        mixed = jnp.dot(s.wmat[k, 0], both_cols, preferred_element_type=F32)
        mixed = mixed + jnp.dot(s.wmat[k, 1], both_cols, preferred_element_type=F32)
        s.macc[0] += mixed[:, 0:128]
        s.macc[1] += mixed[:, 128:256]

    def at(step, lag, stage, count=chunks):
        @pl.when((step >= lag) & (step < lag + count))
        def _():
            stage(step - lag)

    wait_all(s.pre.at[pl.ds(0, 2)], s.p_rs.at[0])
    early_copy(xl, pl.ds(0, n_early // 2), 1, right).start()
    early_copy(xr, pl.ds(n_early // 2, n_early // 2), 1, left).start()

    @pl.loop(0, chunks + LAGS[4])
    def _(step):
        pl.when(step == SEND_EARLY)(leave_early)
        at(step, 0, arrive, late)
        at(step, LAGS[0], forward, late)
        at(step, LAGS[2], pass_on)
        at(step, LAGS[3], finish)
        at(step, LAGS[1], experts_of)
        at(step, LAGS[4], combine)

    s.mix_s[...] = s.macc[oc].astype(BF16)
    mix_copy = remote(s.mix_s, s.mix_r, s.one_ss.at[2], s.one_rs.at[2], partner)
    mix_copy.start()
    own = s.resid[...] + s.macc[mc]
    mix_copy.wait_recv()
    out_ref[...] = (own + s.mix_r[...].astype(F32)).astype(BF16)

    for copy in [gain_copy, resid_copy, mix_copy]:
        copy.wait_send()
    wait_all(s.ybuf, s.w_sem.at[1])
    for phase in range(2):
        wait_all(s.stat_r.at[phase], s.st_ss.at[phase])
    wait_all(s.halo_r, s.edge_ss.at[0])
    wait_all(s.edge_r, s.edge_ss.at[1])
    wait_all(s.gath.at[pl.ds(0, 3), pl.ds(0, late * per)], s.g_ss.at[0])
    wait_all(s.pre.at[pl.ds(0, 3)], s.p_ss.at[0])
    wait_all(s.pre, s.a_ss.at[1])
    wait_all(s.rs_s, s.r_ss.at[0])
    wait_all(s.table.at[pl.ds(0, late * per - 1)], s.a_ss.at[0])
    wait_all(s.back.at[pl.ds(0, chunks * per - 1)], s.b_ss.at[0])

    @pl.when(par > 0)
    def _():
        wait_all(s.table.at[0], s.a_ss.at[0])
        wait_all(s.back.at[0], s.b_ss.at[0])


def shards(frames, conv_kernel, conv_gain, ffn_gain, lengths, routes, route_weights, w_gate, w_up, w_down):
    rows, width = frames.shape
    _, depth, hid = w_gate.shape
    scratch = names(rows, width, hid, depth, conv_kernel.shape[0], lengths.shape[0])
    vmem = pl.BlockSpec(memory_space=pltpu.VMEM)
    return pl.pallas_call(
        functools.partial(kernel, tuple(scratch)),
        out_shape=jax.ShapeDtypeStruct((rows, width), BF16),
        in_specs=[pl.BlockSpec(memory_space=pl.ANY)] * 10,
        out_specs=vmem,
        scratch_shapes=list(scratch.values()),
        compiler_params=pltpu.CompilerParams(collective_id=0, has_side_effects=True, vmem_limit_bytes=56 * 1024 * 1024),
    )(
        lengths,
        frames,
        conv_kernel,
        conv_gain.reshape(1, width),
        ffn_gain.reshape(1, width),
        routes.T,
        route_weights.T,
        w_gate.reshape(depth, hid),
        w_up.reshape(depth, hid),
        w_down.reshape(hid, depth),
    )


def solution(mesh):
    in_specs = (
        P("tm", "tensor"),
        P(None, "tensor"),
        P("tensor"),
        P("tensor"),
        P(),
        P("tm", None),
        P("tm", None),
        P("tm", None, "tensor"),
        P("tm", None, "tensor"),
        P("tm", "tensor", None),
    )
    return jax.shard_map(shards, mesh=mesh, in_specs=in_specs, out_specs=P("tm", "tensor"), check_vma=False)
```
